256 devices in a mesh: row: 8 (over z_lo, core), col: 32 (over y, x, z_hi).
Axes of the slice: x: 4, y: 4, z: 8 (z_hi: 2, z_lo: 4; z = z_hi * 4 + z_lo), core: 2. Of those that a mesh axis runs over, the one named last changes fastest.
Arguments:
- query_vecs: bfloat16 [16384, 1280], P(('row', 'col')), may hold values from -6 to 6
- key_vecs: bfloat16 [16384, 1280], P(('col', 'row')), may hold values from -6 to 6
- value_vecs: bfloat16 [16384, 1280], P(('col', 'row')), may hold values from -6 to 6
- attn_out: bfloat16 [16384, 1280], P(('row', 'col')), may hold values from -6 to 6
- out_grad: bfloat16 [16384, 1280], P(('row', 'col')), may hold values from -180 to 180
- saved_lse: float32 [16384, 16], P(('row', 'col')), may hold values from 9 to 10.5
- kept_mask: int32 [16384], P(('col', 'row')), may hold values from 0 to 1, as said below
Outputs:
- query_grad: bfloat16 [16384, 1280], P(('row', 'col'))
- key_grad: bfloat16 [16384, 1280], P(('col', 'row'))
- value_grad: bfloat16 [16384, 1280], P(('col', 'row'))
The draws below stay inside these ranges and needn't reach their ends.
Inputs may be any that keep to these rules, and one draw needn't show every extreme that they name: `kept_mask`: 1 marks a kept token, 0 a token dropped from the scene.
All inputs are finite; a program needn't handle non-finite values.
Results may differ from the reference program's by a relative error of at most 0.0049.
Values may be sent and summed in bfloat16 or wider, within the bound.
A program may use at most 128 MiB of HBM per device.

```python
import jax
import jax.numpy as jnp
from jax import lax

WIDTH = 1280
HEADS = 16
TOK_DEV = 64
TOKENS = 16384
N_COL = 32


def draw_kept_mask(key, part):
    key = jax.random.fold_in(key, 7)
    first_key, second_key = jax.random.split(key)
    blocks = TOKENS // TOK_DEV
    levels = jax.random.randint(first_key, (blocks, 1), 1, 5)
    throws = jax.random.randint(second_key, (blocks, TOK_DEV), 0, 4)
    return (throws < levels).astype(jnp.int32).reshape(TOKENS)


def shard_levels(own_key, dims, cuts, low, largest):
    loudness, own = 1.0, jax.random.fold_in(own_key, 6)
    for axis_at, parts in cuts:
        draws = jnp.exp(jax.random.uniform(jax.random.fold_in(own, axis_at), (parts,), jnp.float32, low / len(cuts), largest / len(cuts)))
        loudness = loudness * jnp.repeat(draws, dims[axis_at] // parts).reshape([-1 if axis == axis_at else 1 for axis in range(len(dims))])
    return loudness


def normal_values(own_key, dims, spread, bound, shards=(), kind=jnp.bfloat16):
    drawn = spread * jax.random.normal(own_key, dims, jnp.float32)
    if shards:
        drawn = drawn * shard_levels(own_key, dims, shards, -0.22, 0.18)
    return jnp.clip(drawn, -bound, bound).astype(kind)


def setup_inputs(seed: int = 0) -> dict:
    key_of = jax.random.split(jax.random.key(seed), 8)
    return {
        "query_vecs": normal_values(key_of[0], (TOKENS, WIDTH), 1.0, 6.0, ((0, 256),)),
        "key_vecs": normal_values(key_of[1], (TOKENS, WIDTH), 1.0, 6.0, ((0, 256),)),
        "value_vecs": normal_values(key_of[2], (TOKENS, WIDTH), 1.0, 6.0, ((0, 256),)),
        "attn_out": normal_values(key_of[3], (TOKENS, WIDTH), 1.0, 6.0, ((0, 256),)),
        "out_grad": normal_values(key_of[4], (TOKENS, WIDTH), 30.0, 180.0, ((0, 256),)),
        "saved_lse": jnp.clip(9.0 + 1.5 * jax.random.uniform(key_of[5], (TOKENS, HEADS), jnp.float32) ** shard_levels(key_of[5], (TOKENS, HEADS), ((0, 256),), -0.2, 0.2), 9.0, 10.5),
        "kept_mask": draw_kept_mask(jax.random.fold_in(key_of[7], 71), 0),
    }


def reference(query_vecs, key_vecs, value_vecs, attn_out, out_grad, saved_lse, kept_mask):
    tokens, width = query_vecs.shape
    heads = saved_lse.shape[1]
    head_dim = width // heads
    scaling = head_dim ** -0.5
    block = TOK_DEV * N_COL
    blocks = tokens // block
    keep_float = kept_mask.astype(jnp.float32)
    products = out_grad.astype(jnp.float32) * attn_out.astype(jnp.float32)
    delta = jnp.sum(products.reshape(tokens, heads, head_dim), axis=2)

    def split(array):
        return array.reshape(tokens, heads, head_dim).transpose(1, 0, 2)

    def per_head(inputs):
        query_h, key_h, value_h, grad_h, lse_h, delta_h = inputs

        def step(carry, index):
            key_acc, value_acc = carry
            start = index * block
            query_blk = lax.dynamic_slice_in_dim(query_h, start, block, 0)
            grad_blk = lax.dynamic_slice_in_dim(grad_h, start, block, 0)
            lse_blk = lax.dynamic_slice_in_dim(lse_h, start, block, 0)
            delta_blk = lax.dynamic_slice_in_dim(delta_h, start, block, 0)
            scores = jnp.dot(query_blk, key_h.T, preferred_element_type=jnp.float32) * scaling
            probs = keep_float[None, :] * jnp.exp(scores - lse_blk[:, None])
            probs_low = probs.astype(jnp.bfloat16)
            value_acc = value_acc + jnp.dot(probs_low.T, grad_blk, preferred_element_type=jnp.float32)
            grad_probs = jnp.dot(grad_blk, value_h.T, preferred_element_type=jnp.float32)
            grad_scores = (probs * (grad_probs - delta_blk[:, None])).astype(jnp.bfloat16)
            query_part = jnp.dot(grad_scores, key_h, preferred_element_type=jnp.float32) * scaling
            key_acc = key_acc + jnp.dot(grad_scores.T, query_blk, preferred_element_type=jnp.float32)
            return (key_acc, value_acc), query_part

        zeros = jnp.zeros((tokens, head_dim), jnp.float32)
        (key_acc, value_acc), query_parts = lax.scan(step, (zeros, zeros), jnp.arange(blocks, dtype=jnp.int32))
        return query_parts.reshape(tokens, head_dim), key_acc * scaling, value_acc

    query_g, key_g, value_g = lax.map(per_head, (split(query_vecs), split(key_vecs), split(value_vecs), split(out_grad), saved_lse.T, delta.T))

    def merge(array):
        return array.transpose(1, 0, 2).reshape(tokens, width).astype(jnp.bfloat16)

    return merge(query_g), merge(key_g), merge(value_g)
```

```python
import functools

import jax
import jax.numpy as jnp
from jax import lax
from jax.experimental import pallas as pl
from jax.experimental.pallas import tpu as pltpu
from jax.sharding import PartitionSpec as P

HEADS, DIM, TOK = 16, 80, 64
WIDTH = HEADS * DIM
RING = 4
GROUP = HEADS * TOK
TOKENS = RING * GROUP
PAIR = 2 * TOK
QROWS, KROWS, BACK = 96, 80, 128
SCALING = DIM**-0.5
LOG2E = 1.4426950408889634
MESH = pl.DeviceIdType.MESH
F32, BF16 = jnp.float32, jnp.bfloat16
VMEM = pl.BlockSpec(memory_space=pltpu.VMEM)
LIMIT = 56 * 2**20


def place():
    row, col = lax.axis_index("row"), lax.axis_index("col")
    high = lax.rem(col, 2)
    x = lax.rem(lax.div(col, 2), RING)
    y = lax.div(col, 2 * RING)
    return row, col, high * 8 + row, x, y


def head_device(col, head):
    return (lax.rem(head, 8), col - lax.rem(col, 2) + lax.div(head, 8))


def x_device(row, col, x, other):
    return (row, col + 2 * (other - x))


def y_device(row, col, y, other):
    return (row, col + 2 * RING * (other - y))


def greet(devices):
    barrier = pltpu.get_barrier_semaphore()
    for device in devices:
        pl.semaphore_signal(barrier, inc=1, device_id=device, device_id_type=MESH)
    pl.semaphore_wait(barrier, len(devices))


def prepare(q_ref, g_ref, o_ref, k_ref, v_ref, lse_ref, keep_ref, qg_ref, kv_ref):
    def flip(top, bottom):
        return jnp.concatenate([top, bottom], axis=0).astype(F32).T

    lane = lax.broadcasted_iota(jnp.int32, (HEADS, PAIR), 1)
    qg = flip(q_ref[...], g_ref[...])
    both = flip(o_ref[...], o_ref[...])
    delta = jnp.sum((qg * both).reshape(HEADS, DIM, PAIR), axis=1)
    lse = jnp.concatenate([lse_ref[...], jnp.zeros((TOK, HEADS), F32)], axis=0)
    lse = jnp.concatenate([lse, jnp.zeros((PAIR, PAIR - HEADS), F32)], axis=1).T[:HEADS]
    extra = jnp.where(lane < TOK, lse * (1.0 / SCALING), delta)
    first = extra.astype(BF16).astype(F32)
    second = (extra - first).astype(BF16).astype(F32)
    third = extra - first - second
    line = lax.broadcasted_iota(jnp.int32, (QROWS - DIM, PAIR), 0)
    qg_ref[:, :DIM, :] = qg.astype(BF16).reshape(HEADS, DIM, PAIR)
    for head in range(HEADS):
        rows = jnp.where(line == 0, first[head : head + 1], 0.0)
        rows = jnp.where(line == 1, second[head : head + 1], rows)
        rows = jnp.where(line == 2, third[head : head + 1], rows)
        qg_ref[head, DIM:, :] = rows.astype(BF16)
    kv = flip(k_ref[...], v_ref[...]) * keep_ref[...]
    kv_ref[...] = kv.astype(BF16).reshape(HEADS, DIM, PAIR)


def spread(qg_ref, kv_ref, qs_ref, ks_ref, local_sem, send_sem, recv_sem, ring_send, ring_recv):
    row, col, head, x, y = place()
    right, left = lax.rem(x + 1, RING), lax.rem(x + RING - 1, RING)
    up, down = lax.rem(y + 1, RING), lax.rem(y + RING - 1, RING)
    others = [lax.rem(head + step, HEADS) for step in range(1, HEADS)]
    sides = (
        (qs_ref, x, right, left, lambda other: x_device(row, col, x, other)),
        (ks_ref, y, up, down, lambda other: y_device(row, col, y, other)),
    )
    greet(
        [head_device(col, other) for other in others]
        + [find(other) for _, _, after, before, find in sides for other in (after, before)]
    )
    copies = []
    for which, (source, target, at) in enumerate(((qg_ref, qs_ref, x), (kv_ref, ks_ref, y))):
        for number, other in enumerate(others):
            copy = pltpu.make_async_remote_copy(
                src_ref=source.at[other],
                dst_ref=target.at[at, head],
                send_sem=send_sem.at[which, number],
                recv_sem=recv_sem.at[which, number],
                device_id=head_device(col, other),
                device_id_type=MESH,
            )
            copy.start()
            copies.append(copy)
        own = pltpu.make_async_copy(source.at[head], target.at[at, head], local_sem.at[which])
        own.start()
        copies.append(own)
    for copy in copies:
        copy.wait()

    def ring(which, number, ref, part, device):
        copy = pltpu.make_async_remote_copy(
            src_ref=part,
            dst_ref=part,
            send_sem=ring_send.at[which, number],
            recv_sem=ring_recv.at[which, number],
            device_id=device,
            device_id_type=MESH,
        )
        copy.start()
        return copy

    first = []
    for which, (ref, at, after, before, find) in enumerate(sides):
        first.append(
            (
                ring(which, 0, ref, ref.at[at], find(after)),
                ring(which, 1, ref, ref.at[at], find(before)),
            )
        )
    second = []
    half = HEADS // 2
    for which, (ref, at, after, before, find) in enumerate(sides):
        first[which][0].wait()
        second.append(ring(which, 2, ref, ref.at[before, pl.ds(0, half)], find(after)))
        first[which][1].wait()
        second.append(ring(which, 3, ref, ref.at[after, pl.ds(half, half)], find(before)))
    for copy in second:
        copy.wait()


def attend(qs_ref, ks_ref, dq_ref, dk_ref, dv_ref, own_q, own_k, own_v, qa, ga, qt, gt, ka, va, kt, acc):
    _, _, _, x, y = place()
    lane = lax.broadcasted_iota(jnp.int32, (1, PAIR), 1)
    low = lane < TOK

    def split(one, two):
        return (
            jnp.where(low, one, pltpu.roll(two, TOK, 1)),
            jnp.where(low, pltpu.roll(one, TOK, 1), two),
        )

    minus = jnp.where(lax.broadcasted_iota(jnp.int32, (QROWS - DIM, PAIR), 0) < 3, -1.0, 0.0)
    fill = jnp.zeros((PAIR - QROWS, PAIR), F32)

    @pl.loop(0, RING * HEADS // 2)
    def _(pair):
        at = lax.div(pair, HEADS // 2)
        one, two = 2 * lax.rem(pair, HEADS // 2), 2 * lax.rem(pair, HEADS // 2) + 1
        here = pl.ds(pl.multiple_of(pair * PAIR, PAIR), PAIR)
        q, g = split(qs_ref[at, one].astype(F32), qs_ref[at, two].astype(F32))
        qt[:, here] = q[:DIM].astype(BF16)
        gt[:, here] = g[:DIM].astype(BF16)
        qa[here, :] = jnp.concatenate([q, fill], axis=0).T.astype(BF16)
        ga[here, :] = jnp.concatenate([g, fill], axis=0).T.astype(BF16)
        k, v = split(ks_ref[at, one].astype(F32), ks_ref[at, two].astype(F32))
        kt[:, here] = k.astype(BF16)
        ka[:, here] = jnp.concatenate([k, minus, fill], axis=0).astype(BF16)
        va[:, here] = jnp.concatenate([v, minus, fill], axis=0).astype(BF16)

    acc[...] = jnp.zeros_like(acc)
    tq, tk = 1024, 1024

    @pl.loop(0, RING)
    def _(j):
        keys = pl.ds(pl.multiple_of(j * tk, tk), tk)

        def step(i, carry):
            sum_k, sum_v = carry
            queries = pl.ds(pl.multiple_of(i * tq, tq), tq)
            scores = jnp.dot(qa[queries, :], ka[:, keys], preferred_element_type=F32)
            probs = jnp.exp2(scores * (SCALING * LOG2E))
            grad_probs = jnp.dot(ga[queries, :], va[:, keys], preferred_element_type=F32)
            grad_scores = (probs * grad_probs).astype(BF16)
            sum_v = sum_v + jnp.dot(gt[:, queries], probs.astype(BF16), preferred_element_type=F32)
            sum_k = sum_k + jnp.dot(qt[:, queries], grad_scores, preferred_element_type=F32)
            acc[i] += lax.dot_general(
                kt[:, keys], grad_scores, (((1,), (1,)), ((), ())), preferred_element_type=F32
            )
            return sum_k, sum_v

        zeros = jnp.zeros((DIM, tk), F32)
        sum_k, sum_v = lax.fori_loop(0, RING, step, (zeros, zeros))
        dk_ref[j] = sum_k.astype(BF16)
        dv_ref[j] = sum_v.astype(BF16)

        @pl.when(j == y)
        def _():
            own_k[...] = sum_k
            own_v[...] = sum_v

    dq_ref[...] = acc[...].astype(BF16)
    own_q[...] = acc[x]


def collect(
    dq_ref, dk_ref, dv_ref, own_q, own_k, own_v, out_ref,
    got, packed, local_sem, part_send, part_recv, send_sem, recv_sem,
):
    row, col, head, x, y = place()
    others = [lax.rem(head + step, HEADS) for step in range(1, HEADS)]
    xs = [lax.rem(x + step, RING) for step in range(1, RING)]
    ys = [lax.rem(y + step, RING) for step in range(1, RING)]
    greet(
        [head_device(col, other) for other in others]
        + [x_device(row, col, x, other) for other in xs]
        + [y_device(row, col, y, other) for other in ys]
    )
    copies = []
    for which, (ref, places, find) in enumerate(
        (
            (dk_ref, ys, lambda other: y_device(row, col, y, other)),
            (dv_ref, ys, lambda other: y_device(row, col, y, other)),
            (dq_ref, xs, lambda other: x_device(row, col, x, other)),
        )
    ):
        for number, other in enumerate(places):
            copy = pltpu.make_async_remote_copy(
                src_ref=ref.at[other],
                dst_ref=got.at[which, number],
                send_sem=part_send.at[which, number],
                recv_sem=part_recv.at[which, number],
                device_id=find(other),
                device_id_type=MESH,
            )
            copy.start()
            copies.append(copy)
    for copy in copies:
        copy.wait()
    low = lax.broadcasted_iota(jnp.int32, (1, PAIR), 1) < TOK
    fill = jnp.zeros((2 * (BACK - DIM) - DIM, PAIR), F32)

    @pl.loop(0, HEADS // 2)
    def _(pair):
        here = pl.ds(pl.multiple_of(pair * PAIR, PAIR), PAIR)

        def total(which, own):
            value = own[:, here]
            for number in range(RING - 1):
                value = value + got[which, number, :, here].astype(F32)
            return value

        k = total(0, own_k) * SCALING
        v = total(1, own_v)
        q = total(2, own_q) * SCALING
        q_top, q_rest = q[: BACK - DIM], jnp.concatenate([q[BACK - DIM :], fill], axis=0)

        def join(one, two):
            return (
                jnp.where(low, one, pltpu.roll(two, TOK, 1)).astype(BF16),
                jnp.where(low, pltpu.roll(one, TOK, 1), two).astype(BF16),
            )

        kv_one, kv_two = join(k, v)
        q_one, q_two = join(q_top, q_rest)
        packed[2 * pair, :DIM, :] = kv_one
        packed[2 * pair, DIM:, :] = q_one
        packed[2 * pair + 1, :DIM, :] = kv_two
        packed[2 * pair + 1, DIM:, :] = q_two

    copies = []
    for number, other in enumerate(others):
        copy = pltpu.make_async_remote_copy(
            src_ref=packed.at[other],
            dst_ref=out_ref.at[head],
            send_sem=send_sem.at[number],
            recv_sem=recv_sem.at[number],
            device_id=head_device(col, other),
            device_id_type=MESH,
        )
        copy.start()
        copies.append(copy)
    own = pltpu.make_async_copy(packed.at[head], out_ref.at[head], local_sem)
    own.start()
    copies.append(own)
    for copy in copies:
        copy.wait()


def finish(back_ref, keep_ref, dq_ref, dk_ref, dv_ref):
    keep = keep_ref[...]
    keep = keep * pltpu.roll(keep, TOK, 1)
    blocks = back_ref[...].astype(F32)
    kv = blocks[:, :DIM, :].reshape(WIDTH, PAIR) * keep
    kv = kv.T
    dk_ref[...] = kv[:TOK].astype(BF16)
    dv_ref[...] = kv[TOK:].astype(BF16)
    pieces = []
    for head in range(HEADS):
        pieces.append(blocks[head, DIM:, :])
        pieces.append(pltpu.roll(blocks[head, DIM : 3 * DIM - BACK, :], TOK, 1))
    q = jnp.concatenate(pieces, axis=0).T
    dq_ref[...] = q[:TOK].astype(BF16)


def params(**more):
    return pltpu.CompilerParams(vmem_limit_bytes=LIMIT, **more)


def on_device(query_vecs, key_vecs, value_vecs, attn_out, out_grad, saved_lse, kept_mask):
    shape = jax.ShapeDtypeStruct
    keep = jnp.concatenate([kept_mask.astype(F32), jnp.ones((TOK,), F32)]).reshape(1, PAIR)
    qg, kv = pl.pallas_call(
        prepare,
        out_shape=[shape((HEADS, QROWS, PAIR), BF16), shape((HEADS, KROWS, PAIR), BF16)],
        in_specs=[VMEM] * 7,
        out_specs=[VMEM] * 2,
        compiler_params=params(),
    )(query_vecs, out_grad, attn_out, key_vecs, value_vecs, saved_lse, keep)
    qs, ks = pl.pallas_call(
        spread,
        out_shape=[shape((RING, HEADS, QROWS, PAIR), BF16), shape((RING, HEADS, KROWS, PAIR), BF16)],
        in_specs=[VMEM] * 2,
        out_specs=[VMEM] * 2,
        scratch_shapes=[
            pltpu.SemaphoreType.DMA((2,)),
            pltpu.SemaphoreType.DMA((2, HEADS - 1)),
            pltpu.SemaphoreType.DMA((2, HEADS - 1)),
            pltpu.SemaphoreType.DMA((2, 4)),
            pltpu.SemaphoreType.DMA((2, 4)),
        ],
        compiler_params=params(collective_id=0, has_side_effects=True),
    )(qg, kv)
    part = shape((RING, DIM, GROUP), BF16)
    own = shape((DIM, GROUP), F32)
    parts = pl.pallas_call(
        attend,
        out_shape=[part] * 3 + [own] * 3,
        in_specs=[VMEM] * 2,
        out_specs=[VMEM] * 6,
        scratch_shapes=[
            pltpu.VMEM((TOKENS, PAIR), BF16),
            pltpu.VMEM((TOKENS, PAIR), BF16),
            pltpu.VMEM((DIM, TOKENS), BF16),
            pltpu.VMEM((DIM, TOKENS), BF16),
            pltpu.VMEM((PAIR, TOKENS), BF16),
            pltpu.VMEM((PAIR, TOKENS), BF16),
            pltpu.VMEM((DIM, TOKENS), BF16),
            pltpu.VMEM((RING, DIM, GROUP), F32),
        ],
        compiler_params=params(),
    )(qs, ks)
    back = pl.pallas_call(
        collect,
        out_shape=shape((HEADS, BACK, PAIR), BF16),
        in_specs=[VMEM] * 6,
        out_specs=VMEM,
        scratch_shapes=[
            pltpu.VMEM((3, RING - 1, DIM, GROUP), BF16),
            pltpu.VMEM((HEADS, BACK, PAIR), BF16),
            pltpu.SemaphoreType.DMA,
            pltpu.SemaphoreType.DMA((3, RING - 1)),
            pltpu.SemaphoreType.DMA((3, RING - 1)),
            pltpu.SemaphoreType.DMA((HEADS - 1,)),
            pltpu.SemaphoreType.DMA((HEADS - 1,)),
        ],
        compiler_params=params(collective_id=1, has_side_effects=True),
    )(*parts)
    out = shape((TOK, WIDTH), BF16)
    return pl.pallas_call(
        finish,
        out_shape=[out] * 3,
        in_specs=[VMEM] * 2,
        out_specs=[VMEM] * 3,
        compiler_params=params(),
    )(back, keep)


def solution(mesh):
    queries, keys = P(("row", "col"), None), P(("col", "row"), None)
    return jax.shard_map(
        on_device,
        mesh=mesh,
        in_specs=(queries, keys, keys, queries, queries, queries, P(("col", "row"))),
        out_specs=(queries, keys, keys),
        check_vma=False,
    )
```

```python
import jax
import jax.numpy as jnp
from jax import lax
from jax.experimental import pallas as pl
from jax.experimental.pallas import tpu as pltpu
from jax.sharding import PartitionSpec as P

HEADS, DIM, TOK = 16, 80, 64
WIDTH = HEADS * DIM
RING = 4
GROUP = HEADS * TOK
PAIR = 2 * TOK
QUARTER = GROUP // RING
QROWS, TOP = 96, 48
REST = DIM - TOP
SCALING = DIM**-0.5
LOG2E = 1.4426950408889634
MESH = pl.DeviceIdType.MESH
F32, BF16 = jnp.float32, jnp.bfloat16
VMEM = pl.BlockSpec(memory_space=pltpu.VMEM)


def kernel(
    q_ref, g_ref, o_ref, k_ref, v_ref, lse_ref, keep_ref, dq_ref, dk_ref, dv_ref,
    keep, extra, qg, kv, qs, ks, qa, ga, qt, gt, ka, va, kt, acc_q, acc_k, acc_v,
    part_k, got_k, own_k, part_q, got_q, pack_k, pack_q, back_k, back_q,
    local_sem, in_send, in_recv, ring_send, ring_recv,
    sum_send, sum_recv, sumq_send, sumq_recv, out_send, out_recv,
):
    row, col = lax.axis_index("row"), lax.axis_index("col")
    high = lax.rem(col, 2)
    head = high * 8 + row
    x, y = lax.rem(lax.div(col, 2), RING), lax.div(col, 2 * RING)

    def head_device(step):
        other = lax.rem(head + step + HEADS, HEADS)
        return other, (lax.rem(other, 8), col - high + lax.div(other, 8))

    def side_device(which, step):
        if which == 0:
            return (row, col + 2 * (lax.rem(x + step + RING, RING) - x))
        return (row, col + 2 * RING * (lax.rem(y + step + RING, RING) - y))

    def remote(source, target, send, recv, device):
        return pltpu.make_async_remote_copy(
            src_ref=source, dst_ref=target, send_sem=send, recv_sem=recv,
            device_id=device, device_id_type=MESH,
        )

    def arrive(which, step):
        other, device = head_device(step)
        source, target = ((qg, qs), (kv, ks))[which]
        return remote(
            source.at[other], target.at[0, step],
            in_send.at[which, step], in_recv.at[which, step], device,
        )

    def arrive_own(which):
        source, target = ((qg, qs), (kv, ks))[which]
        return pltpu.make_async_copy(source.at[head], target.at[0, 0], local_sem.at[which])

    def ring(which, group, kind):
        ref = (qs, ks)[which]
        source, target, first, count, step = (
            (0, 1, 0, 4, 1), (0, 2, 0, 4, -1), (1, 3, 0, 2, 1), (2, 3, 2, 2, -1),
        )[kind]
        part = pl.ds(4 * group + first, count)
        return remote(
            ref.at[source, part], ref.at[target, part],
            ring_send.at[which, group, kind], ring_recv.at[which, group, kind],
            side_device(which, step),
        )

    back_steps = (-1, 1, 2)

    def sum_keys(quarter, slot):
        return remote(
            part_k.at[quarter, slot], got_k.at[quarter, slot],
            sum_send.at[quarter, slot], sum_recv.at[quarter, slot],
            side_device(1, back_steps[slot]),
        )

    def sum_queries(slot):
        return remote(
            part_q.at[slot], got_q.at[slot], sumq_send.at[slot], sumq_recv.at[slot],
            side_device(0, back_steps[slot]),
        )

    def leave(which, step):
        source, target = ((pack_q, back_q), (pack_k, back_k))[which]
        if step == 0:
            return pltpu.make_async_copy(source.at[0], target.at[head], local_sem.at[2 + which])
        _, device = head_device(-step)
        return remote(
            source.at[step], target.at[head],
            out_send.at[which, step], out_recv.at[which, step], device,
        )

    barrier = pltpu.get_barrier_semaphore()
    partners = [head_device(step)[1] for step in range(1, HEADS)]
    partners += [side_device(which, step) for which in (0, 1) for step in back_steps]
    for device in partners:
        pl.semaphore_signal(barrier, inc=1, device_id=device, device_id_type=MESH)

    def flip(top, bottom):
        return jnp.concatenate([top, bottom], axis=0).astype(F32).T

    keep[...] = jnp.ones_like(keep)
    keep[0:1, :TOK] = keep_ref[...].astype(F32)
    kv[...] = (flip(k_ref[...], v_ref[...]) * keep[0:1, :]).astype(BF16).reshape(HEADS, DIM, PAIR)
    pl.semaphore_wait(barrier, len(partners))
    arrive_own(1).start()
    for step in range(1, 4):
        arrive(1, step).start()

    qg_flat = flip(q_ref[...], g_ref[...])
    o_flat = flip(o_ref[...], o_ref[...])
    delta = jnp.sum((qg_flat * o_flat).reshape(HEADS, DIM, PAIR), axis=1)
    extra[...] = jnp.zeros_like(extra)
    extra[:, :TOK] = lse_ref[...] * (1.0 / SCALING)
    low = lax.broadcasted_iota(jnp.int32, (1, PAIR), 1) < TOK
    whole = jnp.where(low, extra[...], delta)
    first = whole.astype(BF16).astype(F32)
    second = (whole - first).astype(BF16).astype(F32)
    third = whole - first - second
    line = lax.broadcasted_iota(jnp.int32, (QROWS - DIM, PAIR), 0)
    qg[:, :DIM, :] = qg_flat.astype(BF16).reshape(HEADS, DIM, PAIR)
    for number in range(HEADS):
        rows = jnp.where(line == 0, first[number : number + 1], 0.0)
        rows = jnp.where(line == 1, second[number : number + 1], rows)
        rows = jnp.where(line == 2, third[number : number + 1], rows)
        qg[number, DIM:, :] = rows.astype(BF16)
    arrive_own(0).start()
    for step in range(1, HEADS):
        arrive(0, step).start()
    for step in range(4, HEADS):
        arrive(1, step).start()

    def swap(value):
        return pltpu.roll(value, TOK, 1)

    def mix(one, two):
        return jnp.where(low, one, swap(two)), jnp.where(low, swap(one), two)

    minus = jnp.where(line < 3, -1.0, 0.0)
    fill = jnp.zeros((PAIR - QROWS, PAIR), F32)

    def lay_queries(slot, pairs):
        for pair in pairs:
            here = pl.ds(pair * PAIR, PAIR)
            q, g = mix(qs[slot, 2 * pair].astype(F32), qs[slot, 2 * pair + 1].astype(F32))
            qt[slot, :, here] = q[:DIM].astype(BF16)
            gt[slot, :, here] = g[:DIM].astype(BF16)
            qa[slot, here, :] = jnp.concatenate([q, fill], axis=0).T.astype(BF16)
            ga[slot, here, :] = jnp.concatenate([g, fill], axis=0).T.astype(BF16)

    def lay_keys(quarter, slot):
        for pair in range(2):
            here = pl.ds(slot * QUARTER + pair * PAIR, PAIR)
            at = 4 * quarter + 2 * pair
            k, v = mix(ks[slot, at].astype(F32), ks[slot, at + 1].astype(F32))
            kt[quarter, :, here] = k.astype(BF16)
            ka[quarter, :, here] = jnp.concatenate([k, minus, fill], axis=0).astype(BF16)
            va[quarter, :, here] = jnp.concatenate([v, minus, fill], axis=0).astype(BF16)

    def ring_one(which, group):
        for step in range(4 * group, 4 * group + 4):
            if step == 0:
                arrive_own(which).wait()
            else:
                arrive(which, step).wait_recv()
        ring(which, group, 0).start()
        ring(which, group, 1).start()

    def ring_two(which, group):
        ring(which, group, 0).wait_recv()
        ring(which, group, 2).start()
        ring(which, group, 1).wait_recv()
        ring(which, group, 3).start()

    def ring_end(which, group):
        ring(which, group, 2).wait_recv()
        ring(which, group, 3).wait_recv()

    def send_keys(quarter):
        for slot in range(3):
            here = pl.ds((slot + 1) * QUARTER, QUARTER)
            part_k[quarter, slot, 0] = acc_k[:, here].astype(BF16)
            part_k[quarter, slot, 1] = acc_v[:, here].astype(BF16)
            sum_keys(quarter, slot).start()
        own_k[quarter, 0] = acc_k[:, :QUARTER]
        own_k[quarter, 1] = acc_v[:, :QUARTER]
        acc_k[...] = jnp.zeros_like(acc_k)
        acc_v[...] = jnp.zeros_like(acc_v)

    def return_keys(quarter):
        for slot in range(3):
            sum_keys(quarter, slot).wait_recv()
        for pair in range(2):
            here = pl.ds(pair * PAIR, PAIR)
            k, v = [
                own_k[quarter, which, :, here]
                + got_k[quarter, 0, which, :, here].astype(F32)
                + got_k[quarter, 1, which, :, here].astype(F32)
                + got_k[quarter, 2, which, :, here].astype(F32)
                for which in (0, 1)
            ]
            one, two = (k * SCALING), v
            at = 4 * quarter + 2 * pair
            pack_k[at] = jnp.where(low, one, swap(two)).astype(BF16)
            pack_k[at + 1] = jnp.where(low, swap(one), two).astype(BF16)
        for step in range(4 * quarter, 4 * quarter + 4):
            leave(1, step).start()

    def send_queries(slot):
        part_q[slot - 1] = acc_q[slot].astype(BF16)
        sum_queries(slot - 1).start()

    def return_queries():
        for slot in range(3):
            sum_queries(slot).wait_recv()
        for pair in range(HEADS // 2):
            here = pl.ds(pair * PAIR, PAIR)
            q = acc_q[0, :, here]
            for slot in range(3):
                q = q + got_q[slot, :, here].astype(F32)
            q = q * SCALING
            one, two = q[:TOP], jnp.concatenate([q[TOP:], jnp.zeros((TOP - REST, PAIR), F32)], axis=0)
            pack_q[2 * pair] = jnp.where(low, one, swap(two)).astype(BF16)
            pack_q[2 * pair + 1] = jnp.where(low, swap(one), two).astype(BF16)
        for step in range(HEADS):
            leave(0, step).start()

    acc_q[...] = jnp.zeros_like(acc_q)
    acc_k[...] = jnp.zeros_like(acc_k)
    acc_v[...] = jnp.zeros_like(acc_v)
    ring_one(1, 0)
    for group in range(4):
        ring_one(0, group)
        lay_queries(0, (2 * group, 2 * group + 1))
    ring_two(1, 0)
    for slot in range(3):
        lay_keys(0, slot)
    ring_end(1, 0)
    lay_keys(0, 3)

    def before(turn):
        quarter, slot = divmod(turn, 4)
        if turn == 1:
            for group in range(4):
                ring_two(0, group)
            for place in (1, 2):
                lay_queries(place, range(HEADS // 2))
        if turn == 3:
            for group in range(4):
                ring_end(0, group)
            lay_queries(3, range(HEADS // 2))
        if slot == 0 and quarter > 0:
            send_keys(quarter - 1)
            ring_end(1, quarter)
            for place in range(4):
                lay_keys(quarter, place)
        if slot == 1 and quarter < 3:
            ring_one(1, quarter + 1)
        if slot == 2 and quarter < 3:
            ring_two(1, quarter + 1)
        if slot == 2 and quarter > 0:
            return_keys(quarter - 1)
        if quarter == 3 and slot > 0:
            send_queries(slot)

    def tile(turn, carry):
        quarter = lax.div(turn, 4)
        slot = lax.rem(turn + lax.div(quarter, 3), 4)
        for at in range(16):
            if at > 0:
                pl.when(turn == at)(lambda at=at: before(at))
        scores = jnp.dot(qa[slot], ka[quarter], preferred_element_type=F32)
        probs = jnp.exp2(scores * (SCALING * LOG2E))
        grad_probs = jnp.dot(ga[slot], va[quarter], preferred_element_type=F32)
        grad_scores = (probs * grad_probs).astype(BF16)
        acc_v[...] += jnp.dot(gt[slot], probs.astype(BF16), preferred_element_type=F32)
        acc_k[...] += jnp.dot(qt[slot], grad_scores, preferred_element_type=F32)
        acc_q[slot] += lax.dot_general(
            kt[quarter], grad_scores, (((1,), (1,)), ((), ())), preferred_element_type=F32
        )
        return carry

    lax.fori_loop(0, 16, tile, 0)
    send_keys(3)
    return_queries()
    return_keys(3)

    for step in range(HEADS):
        for which in (0, 1):
            if step == 0:
                leave(which, step).wait()
            else:
                leave(which, step).wait_recv()
    both = keep[0:1, :] * swap(keep[...])[0:1, :]
    flat = (back_k[...].astype(F32).reshape(WIDTH, PAIR) * both).T
    dk_ref[...] = flat[:TOK].astype(BF16)
    dv_ref[...] = flat[TOK:].astype(BF16)
    pieces = []
    for number in range(HEADS):
        block = back_q[number].astype(F32)
        pieces += [block, swap(block)[:REST]]
    dq_ref[...] = jnp.concatenate(pieces, axis=0).T[:TOK].astype(BF16)

    for step in range(1, HEADS):
        for which in (0, 1):
            arrive(which, step).wait_send()
            leave(which, step).wait_send()
    for which in (0, 1):
        for group in range(4):
            for kind in range(4):
                ring(which, group, kind).wait_send()
    for slot in range(3):
        sum_queries(slot).wait_send()
        for quarter in range(4):
            sum_keys(quarter, slot).wait_send()


def on_device(query_vecs, key_vecs, value_vecs, attn_out, out_grad, saved_lse, kept_mask):
    out = jax.ShapeDtypeStruct((TOK, WIDTH), BF16)
    dma = pltpu.SemaphoreType.DMA

    def low_bits(*dims):
        return pltpu.VMEM(dims, BF16)

    def full(*dims):
        return pltpu.VMEM(dims, F32)

    return pl.pallas_call(
        kernel,
        out_shape=[out] * 3,
        in_specs=[VMEM] * 7,
        out_specs=[VMEM] * 3,
        scratch_shapes=[
            full(8, PAIR),
            full(HEADS, PAIR),
            low_bits(HEADS, QROWS, PAIR),
            low_bits(HEADS, DIM, PAIR),
            low_bits(RING, HEADS, QROWS, PAIR),
            low_bits(RING, HEADS, DIM, PAIR),
            low_bits(RING, GROUP, PAIR),
            low_bits(RING, GROUP, PAIR),
            low_bits(RING, DIM, GROUP),
            low_bits(RING, DIM, GROUP),
            low_bits(RING, PAIR, GROUP),
            low_bits(RING, PAIR, GROUP),
            low_bits(RING, DIM, GROUP),
            full(RING, DIM, GROUP),
            full(DIM, GROUP),
            full(DIM, GROUP),
            low_bits(RING, 3, 2, DIM, QUARTER),
            low_bits(RING, 3, 2, DIM, QUARTER),
            full(RING, 2, DIM, QUARTER),
            low_bits(3, DIM, GROUP),
            low_bits(3, DIM, GROUP),
            low_bits(HEADS, DIM, PAIR),
            low_bits(HEADS, TOP, PAIR),
            low_bits(HEADS, DIM, PAIR),
            low_bits(HEADS, TOP, PAIR),
            dma((4,)),
            dma((2, HEADS)),
            dma((2, HEADS)),
            dma((2, 4, 4)),
            dma((2, 4, 4)),
            dma((4, 3)),
            dma((4, 3)),
            dma((3,)),
            dma((3,)),
            dma((2, HEADS)),
            dma((2, HEADS)),
        ],
        compiler_params=pltpu.CompilerParams(
            vmem_limit_bytes=56 * 2**20, collective_id=0, has_side_effects=True
        ),
    )(
        query_vecs, out_grad, attn_out, key_vecs, value_vecs, saved_lse.T,
        kept_mask.reshape(1, TOK),
    )


def solution(mesh):
    queries, keys = P(("row", "col"), None), P(("col", "row"), None)
    return jax.shard_map(
        on_device,
        mesh=mesh,
        in_specs=(queries, keys, keys, queries, queries, queries, P(("col", "row"))),
        out_specs=(queries, keys, keys),
        check_vma=False,
    )
```

```python
import jax
import jax.numpy as jnp
from jax import lax
from jax.experimental import pallas as pl
from jax.experimental.pallas import tpu as pltpu
from jax.sharding import PartitionSpec as P

HEADS, DIM, TOK = 16, 80, 64
WIDTH = HEADS * DIM
RING = 4
GROUP = HEADS * TOK
PAIR = 2 * TOK
QUARTER = GROUP // RING
QROWS, TOP = 96, 48
REST = DIM - TOP
SCALING = DIM**-0.5
LOG2E = 1.4426950408889634
MESH = pl.DeviceIdType.MESH
F32, BF16 = jnp.float32, jnp.bfloat16
STEPS = (0, 1, -1, 2, -2, 3, -3, 4, -4, 5, -5, 6, -6, 7, -7, 8)
ORDER = (
    (0, 0), (0, 1), (1, 0), (1, 1), (0, 2), (1, 2), (2, 0), (2, 1), (2, 2),
    (3, 3), (0, 3), (1, 3), (2, 3), (3, 1), (3, 2), (3, 0),
)
QUERY_CODE = sum((3 - q) * 4**turn for turn, (q, _) in enumerate(ORDER))
KEY_CODE = sum(k * 4**turn for turn, (_, k) in enumerate(ORDER))
VMEM = pl.BlockSpec(memory_space=pltpu.VMEM)


def kernel(
    q_ref, g_ref, o_ref, k_ref, v_ref, lse_ref, keep_ref, dq_ref, dk_ref, dv_ref,
    keep, extra, qg, kv, qs, ks, qa, ga, qt, gt, ka, va, kt, acc_q, acc_k, acc_v,
    part_k, got_k, part_q, got_q, pack_k, pack_q, back_k, back_q,
    local_sem, in_send, in_recv, ring_send, ring_recv,
    sum_send, sum_recv, sumq_send, sumq_recv, out_send, out_recv,
):
    row, col = lax.axis_index("row"), lax.axis_index("col")
    high = lax.rem(col, 2)
    head = high * 8 + row
    x, y = lax.rem(lax.div(col, 2), RING), lax.div(col, 2 * RING)

    def head_device(step):
        other = lax.rem(head + step + HEADS, HEADS)
        return other, (lax.rem(other, 8), col - high + lax.div(other, 8))

    def side_device(which, step):
        if which == 0:
            return (row, col + 2 * (lax.rem(x + step + RING, RING) - x))
        return (row, col + 2 * RING * (lax.rem(y + step + RING, RING) - y))

    def remote(source, target, send, recv, device):
        return pltpu.make_async_remote_copy(
            src_ref=source, dst_ref=target, send_sem=send, recv_sem=recv,
            device_id=device, device_id_type=MESH,
        )

    def arrive(which, step):
        other, device = head_device(STEPS[step])
        source, target = ((qg, qs), (kv, ks))[which]
        return remote(
            source.at[other], target.at[0, step],
            in_send.at[which, step], in_recv.at[which, step], device,
        )

    def arrive_own(which):
        source, target = ((qg, qs), (kv, ks))[which]
        return pltpu.make_async_copy(source.at[head], target.at[0, 0], local_sem.at[which])

    def ring(which, group, kind):
        ref = (qs, ks)[which]
        source, target, first, count, step = (
            (0, 1, 0, 4, 1), (0, 2, 0, 4, -1), (1, 3, 0, 2, 1), (2, 3, 2, 2, -1),
        )[kind]
        part = pl.ds(4 * group + first, count)
        return remote(
            ref.at[source, part], ref.at[target, part],
            ring_send.at[which, group, kind], ring_recv.at[which, group, kind],
            side_device(which, step),
        )

    back_steps = (-1, 1, 2)

    def sum_keys(quarter, slot):
        return remote(
            part_k.at[quarter, slot], got_k.at[quarter, slot],
            sum_send.at[quarter, slot], sum_recv.at[quarter, slot],
            side_device(1, back_steps[slot]),
        )

    def sum_queries(quarter, slot):
        return remote(
            part_q.at[quarter, slot], got_q.at[quarter, slot],
            sumq_send.at[quarter, slot], sumq_recv.at[quarter, slot],
            side_device(0, back_steps[slot]),
        )

    def leave(which, step):
        source, target = ((pack_q, back_q), (pack_k, back_k))[which]
        if step == 0:
            return pltpu.make_async_copy(source.at[0], target.at[head], local_sem.at[2 + which])
        _, device = head_device(-STEPS[step])
        return remote(
            source.at[step], target.at[head],
            out_send.at[which, step], out_recv.at[which, step], device,
        )

    barrier = pltpu.get_barrier_semaphore()
    partners = [head_device(step)[1] for step in range(1, HEADS)]
    partners += [side_device(which, step) for which in (0, 1) for step in back_steps]
    for device in partners:
        pl.semaphore_signal(barrier, inc=1, device_id=device, device_id_type=MESH)

    def flip(top, bottom):
        return jnp.concatenate([top, bottom], axis=0).astype(F32).T

    keep[...] = jnp.ones_like(keep)
    keep[0:1, :TOK] = keep_ref[...].astype(F32)
    kv[...] = (flip(k_ref[...], v_ref[...]) * keep[0:1, :]).astype(BF16).reshape(HEADS, DIM, PAIR)

    qg_flat = flip(q_ref[...], g_ref[...])
    o_flat = flip(o_ref[...], o_ref[...])
    delta = jnp.sum((qg_flat * o_flat).reshape(HEADS, DIM, PAIR), axis=1)
    extra[...] = jnp.zeros_like(extra)
    extra[:, :TOK] = lse_ref[...] * (1.0 / SCALING)
    low = lax.broadcasted_iota(jnp.int32, (1, PAIR), 1) < TOK
    whole = jnp.where(low, extra[...], delta)
    first = whole.astype(BF16).astype(F32)
    second = (whole - first).astype(BF16).astype(F32)
    third = whole - first - second
    line = lax.broadcasted_iota(jnp.int32, (QROWS - DIM, PAIR), 0)
    qg[:, :DIM, :] = qg_flat.astype(BF16).reshape(HEADS, DIM, PAIR)
    for number in range(HEADS):
        rows = jnp.where(line == 0, first[number : number + 1], 0.0)
        rows = jnp.where(line == 1, second[number : number + 1], rows)
        rows = jnp.where(line == 2, third[number : number + 1], rows)
        qg[number, DIM:, :] = rows.astype(BF16)
    pl.semaphore_wait(barrier, len(partners))
    for which in (0, 1):
        arrive_own(which).start()
    for group in range(4):
        for which in (0, 1):
            for step in range(max(1, 4 * group), 4 * group + 4):
                arrive(which, step).start()

    def swap(value):
        return pltpu.roll(value, TOK, 1)

    def mix(one, two):
        return jnp.where(low, one, swap(two)), jnp.where(low, swap(one), two)

    minus = jnp.where(line < 3, -1.0, 0.0)
    fill = jnp.zeros((PAIR - QROWS, PAIR), F32)

    def lay_queries(quarter, slot):
        for pair in range(2):
            here = pl.ds(slot * QUARTER + pair * PAIR, PAIR)
            at = 4 * quarter + 2 * pair
            q, g = mix(qs[slot, at].astype(F32), qs[slot, at + 1].astype(F32))
            qt[quarter, :, here] = q[:DIM].astype(BF16)
            gt[quarter, :, here] = g[:DIM].astype(BF16)
            qa[quarter, here, :] = jnp.concatenate([q, fill], axis=0).T.astype(BF16)
            ga[quarter, here, :] = jnp.concatenate([g, fill], axis=0).T.astype(BF16)

    def lay_keys(quarter, slot):
        for pair in range(2):
            here = pl.ds(slot * QUARTER + pair * PAIR, PAIR)
            at = 4 * quarter + 2 * pair
            k, v = mix(ks[slot, at].astype(F32), ks[slot, at + 1].astype(F32))
            kt[quarter, :, here] = k.astype(BF16)
            ka[quarter, :, here] = jnp.concatenate([k, minus, fill], axis=0).astype(BF16)
            va[quarter, :, here] = jnp.concatenate([v, minus, fill], axis=0).astype(BF16)

    def ring_one(group):
        for which in (0, 1):
            for step in range(4 * group, 4 * group + 4):
                if step == 0:
                    arrive_own(which).wait()
                else:
                    arrive(which, step).wait_recv()
            ring(which, group, 0).start()
            ring(which, group, 1).start()

    def ring_two(group):
        for which in (0, 1):
            ring(which, group, 0).wait_recv()
            ring(which, group, 2).start()
            ring(which, group, 1).wait_recv()
            ring(which, group, 3).start()

    def ring_end(group):
        for which in (0, 1):
            ring(which, group, 2).wait_recv()
            ring(which, group, 3).wait_recv()

    def lay(group, slots):
        for slot in slots:
            lay_queries(group, slot)
            lay_keys(group, slot)

    def send_keys(quarter):
        for slot in range(3):
            here = pl.ds((slot + 1) * QUARTER, QUARTER)
            part_k[quarter, slot, 0] = acc_k[quarter, :, here].astype(BF16)
            part_k[quarter, slot, 1] = acc_v[quarter, :, here].astype(BF16)
            sum_keys(quarter, slot).start()

    def send_queries(quarter):
        for slot in range(3):
            here = pl.ds((slot + 1) * QUARTER, QUARTER)
            part_q[quarter, slot] = acc_q[quarter, :, here].astype(BF16)
            sum_queries(quarter, slot).start()

    def return_keys(quarter):
        for slot in range(3):
            sum_keys(quarter, slot).wait_recv()
        for pair in range(2):
            here = pl.ds(pair * PAIR, PAIR)
            k, v = acc_k[quarter, :, here], acc_v[quarter, :, here]
            for slot in range(3):
                k = k + got_k[quarter, slot, 0, :, here].astype(F32)
                v = v + got_k[quarter, slot, 1, :, here].astype(F32)
            one, two = mix(k * SCALING, v)
            at = 4 * quarter + 2 * pair
            pack_k[at] = one.astype(BF16)
            pack_k[at + 1] = two.astype(BF16)
        for step in range(4 * quarter, 4 * quarter + 4):
            leave(1, step).start()

    def return_queries(quarter):
        for slot in range(3):
            sum_queries(quarter, slot).wait_recv()
        for pair in range(2):
            here = pl.ds(pair * PAIR, PAIR)
            q = acc_q[quarter, :, here]
            for slot in range(3):
                q = q + got_q[quarter, slot, :, here].astype(F32)
            q = q * SCALING
            rest = jnp.concatenate([q[TOP:], jnp.zeros((TOP - REST, PAIR), F32)], axis=0)
            one, two = mix(q[:TOP], rest)
            at = 4 * quarter + 2 * pair
            pack_q[at] = one.astype(BF16)
            pack_q[at + 1] = two.astype(BF16)
        for step in range(4 * quarter, 4 * quarter + 4):
            leave(0, step).start()

    acc_q[...] = jnp.zeros_like(acc_q)
    acc_k[...] = jnp.zeros_like(acc_k)
    acc_v[...] = jnp.zeros_like(acc_v)
    ring_one(0)
    lay(0, (0,))
    ring_two(0)
    lay(0, (1, 2))
    ring_one(1)
    ring_end(0)
    lay(0, (3,))

    def before(turn):
        if turn == 1:
            ring_two(1)
            ring_one(2)
            lay(1, (0, 1, 2))
            ring_end(1)
            lay(1, (3,))
        if turn == 2:
            ring_two(2)
        if turn == 3:
            ring_one(3)
        if turn == 4:
            ring_end(2)
            lay(2, range(4))
        if turn == 5:
            ring_two(3)
        if turn == 9:
            ring_end(3)
            lay(3, range(4))
        if turn == 11:
            send_queries(0)
        if turn == 12:
            send_queries(1)
        if turn == 13:
            send_keys(3)
            send_queries(2)
            return_queries(0)
        if turn == 14:
            send_keys(1)
            return_queries(1)
        if turn == 15:
            send_keys(2)
            return_keys(3)
            return_queries(2)

    def tile(turn, codes):
        code_q, code_k = codes
        query, key = 3 - lax.rem(code_q, 4), lax.rem(code_k, 4)
        for at in range(1, 16):
            pl.when(turn == at)(lambda at=at: before(at))
        scores = jnp.dot(qa[query], ka[key], preferred_element_type=F32)
        probs = jnp.exp2(scores * (SCALING * LOG2E))
        grad_probs = jnp.dot(ga[query], va[key], preferred_element_type=F32)
        grad_scores = (probs * grad_probs).astype(BF16)
        acc_v[key] += jnp.dot(gt[query], probs.astype(BF16), preferred_element_type=F32)
        acc_k[key] += jnp.dot(qt[query], grad_scores, preferred_element_type=F32)
        acc_q[query] += lax.dot_general(
            kt[key], grad_scores, (((1,), (1,)), ((), ())), preferred_element_type=F32
        )
        return lax.div(code_q, 4), lax.div(code_k, 4)

    lax.fori_loop(0, 16, tile, (jnp.int32(QUERY_CODE), jnp.int32(KEY_CODE)))
    send_keys(0)
    send_queries(3)
    return_keys(1)
    return_keys(2)
    return_queries(3)
    return_keys(0)

    for step in range(HEADS):
        for which in (0, 1):
            if step == 0:
                leave(which, step).wait()
            else:
                leave(which, step).wait_recv()
    both = keep[0:1, :] * swap(keep[...])[0:1, :]
    flat = (back_k[...].astype(F32).reshape(WIDTH, PAIR) * both).T
    dk_ref[...] = flat[:TOK].astype(BF16)
    dv_ref[...] = flat[TOK:].astype(BF16)
    pieces = []
    for number in range(HEADS):
        block = back_q[number].astype(F32)
        pieces += [block, swap(block)[:REST]]
    dq_ref[...] = jnp.concatenate(pieces, axis=0).T[:TOK].astype(BF16)

    for step in range(1, HEADS):
        for which in (0, 1):
            arrive(which, step).wait_send()
            leave(which, step).wait_send()
    for which in (0, 1):
        for group in range(4):
            for kind in range(4):
                ring(which, group, kind).wait_send()
    for slot in range(3):
        for quarter in range(4):
            sum_queries(quarter, slot).wait_send()
            sum_keys(quarter, slot).wait_send()


def on_device(query_vecs, key_vecs, value_vecs, attn_out, out_grad, saved_lse, kept_mask):
    out = jax.ShapeDtypeStruct((TOK, WIDTH), BF16)
    dma = pltpu.SemaphoreType.DMA

    def low_bits(*dims):
        return pltpu.VMEM(dims, BF16)

    def full(*dims):
        return pltpu.VMEM(dims, F32)

    return pl.pallas_call(
        kernel,
        out_shape=[out] * 3,
        in_specs=[VMEM] * 7,
        out_specs=[VMEM] * 3,
        scratch_shapes=[
            full(8, PAIR),
            full(HEADS, PAIR),
            low_bits(HEADS, QROWS, PAIR),
            low_bits(HEADS, DIM, PAIR),
            low_bits(RING, HEADS, QROWS, PAIR),
            low_bits(RING, HEADS, DIM, PAIR),
            low_bits(RING, GROUP, PAIR),
            low_bits(RING, GROUP, PAIR),
            low_bits(RING, DIM, GROUP),
            low_bits(RING, DIM, GROUP),
            low_bits(RING, PAIR, GROUP),
            low_bits(RING, PAIR, GROUP),
            low_bits(RING, DIM, GROUP),
            full(RING, DIM, GROUP),
            full(RING, DIM, GROUP),
            full(RING, DIM, GROUP),
            low_bits(RING, 3, 2, DIM, QUARTER),
            low_bits(RING, 3, 2, DIM, QUARTER),
            low_bits(RING, 3, DIM, QUARTER),
            low_bits(RING, 3, DIM, QUARTER),
            low_bits(HEADS, DIM, PAIR),
            low_bits(HEADS, TOP, PAIR),
            low_bits(HEADS, DIM, PAIR),
            low_bits(HEADS, TOP, PAIR),
            dma((4,)),
            dma((2, HEADS)),
            dma((2, HEADS)),
            dma((2, 4, 4)),
            dma((2, 4, 4)),
            dma((4, 3)),
            dma((4, 3)),
            dma((4, 3)),
            dma((4, 3)),
            dma((2, HEADS)),
            dma((2, HEADS)),
        ],
        compiler_params=pltpu.CompilerParams(
            vmem_limit_bytes=56 * 2**20, collective_id=0, has_side_effects=True
        ),
    )(
        query_vecs, out_grad, attn_out, key_vecs, value_vecs, saved_lse.T,
        kept_mask.reshape(1, TOK),
    )


def solution(mesh):
    queries, keys = P(("row", "col"), None), P(("col", "row"), None)
    return jax.shard_map(
        on_device,
        mesh=mesh,
        in_specs=(queries, keys, keys, queries, queries, queries, P(("col", "row"))),
        out_specs=(queries, keys, keys),
        check_vma=False,
    )
```

```python
import jax
import jax.numpy as jnp
from jax import lax
from jax.experimental import pallas as pl
from jax.experimental.pallas import tpu as pltpu
from jax.sharding import PartitionSpec as P

HEADS, DIM, TOK = 16, 80, 64
WIDTH = HEADS * DIM
RING = 4
GROUP = HEADS * TOK
PAIR = 2 * TOK
QUARTER = GROUP // RING
QROWS, TOP = 96, 48
REST = DIM - TOP
SCALING = DIM**-0.5
LOG2E = 1.4426950408889634
MESH = pl.DeviceIdType.MESH
F32, BF16 = jnp.float32, jnp.bfloat16
STEPS = (0, 1, -1, 2, -2, 3, -3, 4, -4, 5, -5, 6, -6, 7, -7, 8)
ROWS, COLUMNS = 256, 512
ORDER = (
    (0, 0), (0, 1), (1, 0), (1, 1), (0, 2), (1, 2), (2, 0), (2, 1), (2, 2),
    (3, 3), (0, 3), (1, 3), (2, 3), (3, 1), (3, 2), (3, 0),
)
VMEM = pl.BlockSpec(memory_space=pltpu.VMEM)


def kernel(
    q_ref, g_ref, o_ref, k_ref, v_ref, lse_ref, keep_ref, back_k, back_q,
    keep, extra, qg, kv, qs, ks, qa, ga, qt, gt, ka, va, kt, acc_q, acc_k, acc_v,
    part_k, got_k, part_q, got_q, pack_k, pack_q,
    local_sem, in_send, in_recv, ring_send, ring_recv,
    sum_send, sum_recv, sumq_send, sumq_recv, out_send, out_recv,
):
    row, col = lax.axis_index("row"), lax.axis_index("col")
    high = lax.rem(col, 2)
    head = high * 8 + row
    x, y = lax.rem(lax.div(col, 2), RING), lax.div(col, 2 * RING)

    def head_device(step):
        other = lax.rem(head + step + HEADS, HEADS)
        return other, (lax.rem(other, 8), col - high + lax.div(other, 8))

    def side_device(which, step):
        if which == 0:
            return (row, col + 2 * (lax.rem(x + step + RING, RING) - x))
        return (row, col + 2 * RING * (lax.rem(y + step + RING, RING) - y))

    def remote(source, target, send, recv, device):
        return pltpu.make_async_remote_copy(
            src_ref=source, dst_ref=target, send_sem=send, recv_sem=recv,
            device_id=device, device_id_type=MESH,
        )

    def arrive(which, step):
        other, device = head_device(STEPS[step])
        source, target = ((qg, qs), (kv, ks))[which]
        return remote(
            source.at[other], target.at[0, step],
            in_send.at[which, step], in_recv.at[which, step], device,
        )

    def arrive_own(which):
        source, target = ((qg, qs), (kv, ks))[which]
        return pltpu.make_async_copy(source.at[head], target.at[0, 0], local_sem.at[which])

    def ring(which, group, kind):
        ref = (qs, ks)[which]
        source, target, first, count, step = (
            (0, 1, 0, 4, 1), (0, 2, 0, 4, -1), (1, 3, 0, 2, 1), (2, 3, 2, 2, -1),
        )[kind]
        part = pl.ds(4 * group + first, count)
        return remote(
            ref.at[source, part], ref.at[target, part],
            ring_send.at[which, group, kind], ring_recv.at[which, group, kind],
            side_device(which, step),
        )

    back_steps = (-1, 1, 2)

    def sum_keys(quarter, slot):
        return remote(
            part_k.at[quarter, slot], got_k.at[quarter, slot],
            sum_send.at[quarter, slot], sum_recv.at[quarter, slot],
            side_device(1, back_steps[slot]),
        )

    def sum_queries(quarter, slot):
        return remote(
            part_q.at[quarter, slot], got_q.at[quarter, slot],
            sumq_send.at[quarter, slot], sumq_recv.at[quarter, slot],
            side_device(0, back_steps[slot]),
        )

    def leave(which, step):
        source, target = ((pack_q, back_q), (pack_k, back_k))[which]
        if step == 0:
            return pltpu.make_async_copy(source.at[0], target.at[head], local_sem.at[2 + which])
        _, device = head_device(-STEPS[step])
        return remote(
            source.at[step], target.at[head],
            out_send.at[which, step], out_recv.at[which, step], device,
        )

    barrier = pltpu.get_barrier_semaphore()
    partners = [head_device(step)[1] for step in range(1, HEADS)]
    partners += [side_device(which, step) for which in (0, 1) for step in back_steps]
    for device in partners:
        pl.semaphore_signal(barrier, inc=1, device_id=device, device_id_type=MESH)

    def flip(top, bottom):
        return jnp.concatenate([top, bottom], axis=0).astype(F32).T

    keep[...] = jnp.ones_like(keep)
    keep[0:1, :TOK] = keep_ref[...].astype(F32)
    kv[...] = (flip(k_ref[...], v_ref[...]) * keep[0:1, :]).astype(BF16).reshape(HEADS, DIM, PAIR)

    qg_flat = flip(q_ref[...], g_ref[...])
    o_flat = flip(o_ref[...], o_ref[...])
    delta = jnp.sum((qg_flat * o_flat).reshape(HEADS, DIM, PAIR), axis=1)
    extra[...] = jnp.zeros_like(extra)
    extra[:, :TOK] = lse_ref[...] * (1.0 / SCALING)
    low = lax.broadcasted_iota(jnp.int32, (1, PAIR), 1) < TOK
    whole = jnp.where(low, extra[...], delta)
    first = whole.astype(BF16).astype(F32)
    second = (whole - first).astype(BF16).astype(F32)
    third = whole - first - second
    line = lax.broadcasted_iota(jnp.int32, (QROWS - DIM, PAIR), 0)
    qg[:, :DIM, :] = qg_flat.astype(BF16).reshape(HEADS, DIM, PAIR)
    for number in range(HEADS):
        rows = jnp.where(line == 0, first[number : number + 1], 0.0)
        rows = jnp.where(line == 1, second[number : number + 1], rows)
        rows = jnp.where(line == 2, third[number : number + 1], rows)
        qg[number, DIM:, :] = rows.astype(BF16)
    pl.semaphore_wait(barrier, len(partners))
    for which in (0, 1):
        arrive_own(which).start()
    for group in range(4):
        for which in (0, 1):
            for step in range(max(1, 4 * group), 4 * group + 4):
                arrive(which, step).start()

    def swap(value):
        return pltpu.roll(value, TOK, 1)

    def mix(one, two):
        return jnp.where(low, one, swap(two)), jnp.where(low, swap(one), two)

    minus = jnp.where(line < 3, -1.0, 0.0)
    fill = jnp.zeros((PAIR - QROWS, PAIR), F32)

    def lay_queries(quarter, slot):
        for pair in range(2):
            here = pl.ds(slot * QUARTER + pair * PAIR, PAIR)
            at = 4 * quarter + 2 * pair
            q, g = mix(qs[slot, at].astype(F32), qs[slot, at + 1].astype(F32))
            qt[quarter, :, here] = q[:DIM].astype(BF16)
            gt[quarter, :, here] = g[:DIM].astype(BF16)
            qa[quarter, here, :] = jnp.concatenate([q, fill], axis=0).T.astype(BF16)
            ga[quarter, here, :] = jnp.concatenate([g, fill], axis=0).T.astype(BF16)

    def lay_keys(quarter, slot):
        for pair in range(2):
            here = pl.ds(slot * QUARTER + pair * PAIR, PAIR)
            at = 4 * quarter + 2 * pair
            k, v = mix(ks[slot, at].astype(F32), ks[slot, at + 1].astype(F32))
            kt[quarter, :, here] = k.astype(BF16)
            ka[quarter, :, here] = jnp.concatenate([k, minus, fill], axis=0).astype(BF16)
            va[quarter, :, here] = jnp.concatenate([v, minus, fill], axis=0).astype(BF16)

    def ring_one(group):
        for which in (0, 1):
            for step in range(4 * group, 4 * group + 4):
                if step == 0:
                    arrive_own(which).wait()
                else:
                    arrive(which, step).wait_recv()
            ring(which, group, 0).start()
            ring(which, group, 1).start()

    def ring_two(group):
        for which in (0, 1):
            ring(which, group, 0).wait_recv()
            ring(which, group, 2).start()
            ring(which, group, 1).wait_recv()
            ring(which, group, 3).start()

    def ring_end(group):
        for which in (0, 1):
            ring(which, group, 2).wait_recv()
            ring(which, group, 3).wait_recv()

    def lay(group, slots):
        for slot in slots:
            lay_queries(group, slot)
            lay_keys(group, slot)

    def send_keys(quarter):
        for slot in range(3):
            here = pl.ds((slot + 1) * QUARTER, QUARTER)
            part_k[quarter, slot, 0] = acc_k[quarter, :, here].astype(BF16)
            part_k[quarter, slot, 1] = acc_v[quarter, :, here].astype(BF16)
            sum_keys(quarter, slot).start()

    def send_queries(quarter):
        for slot in range(3):
            here = pl.ds((slot + 1) * QUARTER, QUARTER)
            part_q[quarter, slot] = acc_q[quarter, :, here].astype(BF16)
            sum_queries(quarter, slot).start()

    def return_keys(quarter):
        for slot in range(3):
            sum_keys(quarter, slot).wait_recv()
        for pair in range(2):
            here = pl.ds(pair * PAIR, PAIR)
            k, v = acc_k[quarter, :, here], acc_v[quarter, :, here]
            for slot in range(3):
                k = k + got_k[quarter, slot, 0, :, here].astype(F32)
                v = v + got_k[quarter, slot, 1, :, here].astype(F32)
            one, two = mix(k * SCALING, v)
            at = 4 * quarter + 2 * pair
            pack_k[at] = one.astype(BF16)
            pack_k[at + 1] = two.astype(BF16)
        for step in range(4 * quarter, 4 * quarter + 4):
            leave(1, step).start()

    def return_queries(quarter):
        for slot in range(3):
            sum_queries(quarter, slot).wait_recv()
        for pair in range(2):
            here = pl.ds(pair * PAIR, PAIR)
            q = acc_q[quarter, :, here]
            for slot in range(3):
                q = q + got_q[quarter, slot, :, here].astype(F32)
            q = q * SCALING
            rest = jnp.concatenate([q[TOP:], jnp.zeros((TOP - REST, PAIR), F32)], axis=0)
            one, two = mix(q[:TOP], rest)
            at = 4 * quarter + 2 * pair
            pack_q[at] = one.astype(BF16)
            pack_q[at + 1] = two.astype(BF16)
        for step in range(4 * quarter, 4 * quarter + 4):
            leave(0, step).start()

    ring_one(0)
    lay(0, (0,))
    ring_two(0)
    lay(0, (1, 2))
    ring_one(1)
    ring_end(0)
    lay(0, (3,))

    def before(turn):
        if turn == 1:
            ring_two(1)
            ring_one(2)
            lay(1, (0, 1, 2))
            ring_end(1)
            lay(1, (3,))
        if turn == 2:
            ring_two(2)
        if turn == 3:
            ring_one(3)
        if turn == 4:
            ring_end(2)
            lay(2, range(4))
        if turn == 5:
            ring_two(3)
        if turn == 9:
            ring_end(3)
            lay(3, range(4))
        if turn == 11:
            send_queries(0)
        if turn == 12:
            send_queries(1)
        if turn == 13:
            send_keys(3)
            send_queries(2)
            return_queries(0)
        if turn == 14:
            send_keys(1)
            return_queries(1)
        if turn == 15:
            send_keys(2)
            return_keys(3)
            return_queries(2)

    def score(chunk):
        query, key, rows, columns = chunk
        scores = jnp.dot(qa[query, rows, :], ka[key, :, columns], preferred_element_type=F32)
        grad_probs = jnp.dot(ga[query, rows, :], va[key, :, columns], preferred_element_type=F32)
        return scores, grad_probs

    def weigh(scores, grad_probs):
        probs = jnp.exp2(scores * (SCALING * LOG2E))
        return probs.astype(BF16), (probs * grad_probs).astype(BF16)

    def gather(chunk, probs, grad_scores):
        query, key, rows, columns = chunk
        parts = (
            (acc_v, key, columns, jnp.dot(gt[query, :, rows], probs, preferred_element_type=F32)),
            (acc_k, key, columns, jnp.dot(qt[query, :, rows], grad_scores, preferred_element_type=F32)),
            (acc_q, query, rows, lax.dot_general(
                kt[key, :, columns], grad_scores, (((1,), (1,)), ((), ())), preferred_element_type=F32
            )),
        )
        for number, (ref, quarter, lanes, part) in enumerate(parts):
            place = (number, quarter, lanes.start)
            ref[quarter, :, lanes] = ref[quarter, :, lanes] + part if place in begun else part
            begun.add(place)

    begun = set()

    def tile(query, key):
        chunks = [
            (query, key, pl.ds(at, ROWS), pl.ds(to, COLUMNS))
            for at in range(0, GROUP, ROWS)
            for to in range(0, GROUP, COLUMNS)
        ]
        ready, waiting = score(chunks[0]), None
        for number, chunk in enumerate(chunks):
            coming = score(chunks[number + 1]) if number + 1 < len(chunks) else None
            weighed = weigh(*ready)
            if waiting is not None:
                gather(chunks[number - 1], *waiting)
            waiting, ready = weighed, coming
        gather(chunks[-1], *waiting)

    for turn, place in enumerate(ORDER):
        before(turn)
        tile(*place)
    send_keys(0)
    send_queries(3)
    return_keys(1)
    return_keys(2)
    return_queries(3)
    return_keys(0)

    for step in range(HEADS):
        for which in (0, 1):
            if step == 0:
                leave(which, step).wait()
            else:
                leave(which, step).wait_recv()
    for step in range(1, HEADS):
        for which in (0, 1):
            arrive(which, step).wait_send()
            leave(which, step).wait_send()
    for which in (0, 1):
        for group in range(4):
            for kind in range(4):
                ring(which, group, kind).wait_send()
    for slot in range(3):
        for quarter in range(4):
            sum_queries(quarter, slot).wait_send()
            sum_keys(quarter, slot).wait_send()


def finish(back_k, back_q, keep_ref, dq_ref, dk_ref, dv_ref, keep):
    keep[:, :TOK] = jnp.broadcast_to(keep_ref[...].astype(F32), (8, TOK))
    keep[:, TOK:] = jnp.broadcast_to(keep_ref[...].astype(F32), (8, TOK))
    flat = (back_k[...].astype(F32).reshape(WIDTH, PAIR) * keep[0:1, :]).T
    dk_ref[...] = flat[:TOK].astype(BF16)
    dv_ref[...] = flat[TOK:].astype(BF16)
    pieces = []
    for number in range(HEADS):
        block = back_q[number].astype(F32)
        pieces += [block, pltpu.roll(block, TOK, 1)[:REST]]
    dq_ref[...] = jnp.concatenate(pieces, axis=0).T[:TOK].astype(BF16)


def on_device(query_vecs, key_vecs, value_vecs, attn_out, out_grad, saved_lse, kept_mask):
    shape = jax.ShapeDtypeStruct
    keep = kept_mask.reshape(1, TOK)
    dma = pltpu.SemaphoreType.DMA

    def low_bits(*dims):
        return pltpu.VMEM(dims, BF16)

    def full(*dims):
        return pltpu.VMEM(dims, F32)

    back = pl.pallas_call(
        kernel,
        out_shape=[shape((HEADS, DIM, PAIR), BF16), shape((HEADS, TOP, PAIR), BF16)],
        in_specs=[VMEM] * 7,
        out_specs=[VMEM] * 2,
        scratch_shapes=[
            full(8, PAIR),
            full(HEADS, PAIR),
            low_bits(HEADS, QROWS, PAIR),
            low_bits(HEADS, DIM, PAIR),
            low_bits(RING, HEADS, QROWS, PAIR),
            low_bits(RING, HEADS, DIM, PAIR),
            low_bits(RING, GROUP, PAIR),
            low_bits(RING, GROUP, PAIR),
            low_bits(RING, DIM, GROUP),
            low_bits(RING, DIM, GROUP),
            low_bits(RING, PAIR, GROUP),
            low_bits(RING, PAIR, GROUP),
            low_bits(RING, DIM, GROUP),
            full(RING, DIM, GROUP),
            full(RING, DIM, GROUP),
            full(RING, DIM, GROUP),
            low_bits(RING, 3, 2, DIM, QUARTER),
            low_bits(RING, 3, 2, DIM, QUARTER),
            low_bits(RING, 3, DIM, QUARTER),
            low_bits(RING, 3, DIM, QUARTER),
            low_bits(HEADS, DIM, PAIR),
            low_bits(HEADS, TOP, PAIR),
            dma((4,)),
            dma((2, HEADS)),
            dma((2, HEADS)),
            dma((2, 4, 4)),
            dma((2, 4, 4)),
            dma((4, 3)),
            dma((4, 3)),
            dma((4, 3)),
            dma((4, 3)),
            dma((2, HEADS)),
            dma((2, HEADS)),
        ],
        compiler_params=pltpu.CompilerParams(
            vmem_limit_bytes=56 * 2**20, collective_id=0, has_side_effects=True
        ),
    )(
        query_vecs, out_grad, attn_out, key_vecs, value_vecs, saved_lse.T, keep,
    )
    return pl.pallas_call(
        finish,
        out_shape=[shape((TOK, WIDTH), BF16)] * 3,
        in_specs=[VMEM] * 3,
        out_specs=[VMEM] * 3,
        scratch_shapes=[full(8, PAIR)],
    )(*back, keep)


def solution(mesh):
    queries, keys = P(("row", "col"), None), P(("col", "row"), None)
    return jax.shard_map(
        on_device,
        mesh=mesh,
        in_specs=(queries, keys, keys, queries, queries, queries, P(("col", "row"))),
        out_specs=(queries, keys, keys),
        check_vma=False,
    )
```

```python
import jax
import jax.numpy as jnp
from jax import lax
from jax.experimental import pallas as pl
from jax.experimental.pallas import tpu as pltpu
from jax.sharding import PartitionSpec as P

HEADS, DIM, TOK = 16, 80, 64
WIDTH = HEADS * DIM
RING = 4
GROUP = HEADS * TOK
PAIR = 2 * TOK
QUARTER = GROUP // RING
QROWS, TOP = 96, 48
REST = DIM - TOP
SCALING = DIM**-0.5
LOG2E = 1.4426950408889634
MESH = pl.DeviceIdType.MESH
F32, BF16 = jnp.float32, jnp.bfloat16
STEPS = (0, 1, -1, 2, -2, 3, -3, 4, -4, 5, -5, 6, -6, 7, -7, 8)
ROWS, COLUMNS = 256, 512
ORDER = (
    (0, 0), (0, 1), (1, 0), (1, 1), (0, 2), (1, 2), (2, 0), (2, 1), (2, 2),
    (3, 3), (0, 3), (1, 3), (2, 3), (3, 1), (3, 2), (3, 0),
)
QUERY_CODE = sum((3 - q) * 4**turn for turn, (q, _) in enumerate(ORDER))
KEY_CODE = sum(k * 4**turn for turn, (_, k) in enumerate(ORDER))
EVENTS = (1, 2, 3, 4, 5, 9, 11, 12, 13, 14, 15)
VMEM = pl.BlockSpec(memory_space=pltpu.VMEM)


def kernel(
    q_ref, g_ref, o_ref, k_ref, v_ref, lse_ref, keep_ref, back_k, back_q,
    keep, extra, qg, kv, qs, ks, qa, ga, qt, gt, ka, va, kt, acc_q, acc_k, acc_v,
    part_k, got_k, part_q, got_q, pack_k, pack_q,
    local_sem, in_send, in_recv, ring_send, ring_recv,
    sum_send, sum_recv, sumq_send, sumq_recv, out_send, out_recv,
):
    row, col = lax.axis_index("row"), lax.axis_index("col")
    high = lax.rem(col, 2)
    head = high * 8 + row
    x, y = lax.rem(lax.div(col, 2), RING), lax.div(col, 2 * RING)

    def head_device(step):
        other = lax.rem(head + step + HEADS, HEADS)
        return other, (lax.rem(other, 8), col - high + lax.div(other, 8))

    def side_device(which, step):
        if which == 0:
            return (row, col + 2 * (lax.rem(x + step + RING, RING) - x))
        return (row, col + 2 * RING * (lax.rem(y + step + RING, RING) - y))

    def remote(source, target, send, recv, device):
        return pltpu.make_async_remote_copy(
            src_ref=source, dst_ref=target, send_sem=send, recv_sem=recv,
            device_id=device, device_id_type=MESH,
        )

    def arrive(which, step):
        other, device = head_device(STEPS[step])
        source, target = ((qg, qs), (kv, ks))[which]
        return remote(
            source.at[other], target.at[0, step],
            in_send.at[which, step], in_recv.at[which, step], device,
        )

    def arrive_own(which):
        source, target = ((qg, qs), (kv, ks))[which]
        return pltpu.make_async_copy(source.at[head], target.at[0, 0], local_sem.at[which])

    def ring(which, group, kind):
        ref = (qs, ks)[which]
        source, target, first, count, step = (
            (0, 1, 0, 4, 1), (0, 2, 0, 4, -1), (1, 3, 0, 2, 1), (2, 3, 2, 2, -1),
        )[kind]
        part = pl.ds(4 * group + first, count)
        return remote(
            ref.at[source, part], ref.at[target, part],
            ring_send.at[which, group, kind], ring_recv.at[which, group, kind],
            side_device(which, step),
        )

    back_steps = (-1, 1, 2)

    def sum_keys(quarter, slot):
        return remote(
            part_k.at[quarter, slot], got_k.at[quarter, slot],
            sum_send.at[quarter, slot], sum_recv.at[quarter, slot],
            side_device(1, back_steps[slot]),
        )

    def sum_queries(quarter, slot):
        return remote(
            part_q.at[quarter, slot], got_q.at[quarter, slot],
            sumq_send.at[quarter, slot], sumq_recv.at[quarter, slot],
            side_device(0, back_steps[slot]),
        )

    def leave(which, step):
        source, target = ((pack_q, back_q), (pack_k, back_k))[which]
        if step == 0:
            return pltpu.make_async_copy(source.at[0], target.at[head], local_sem.at[2 + which])
        _, device = head_device(-STEPS[step])
        return remote(
            source.at[step], target.at[head],
            out_send.at[which, step], out_recv.at[which, step], device,
        )

    barrier = pltpu.get_barrier_semaphore()
    partners = [head_device(step)[1] for step in range(1, HEADS)]
    partners += [side_device(which, step) for which in (0, 1) for step in back_steps]
    for device in partners:
        pl.semaphore_signal(barrier, inc=1, device_id=device, device_id_type=MESH)

    def flip(top, bottom):
        return jnp.concatenate([top, bottom], axis=0).astype(F32).T

    keep[...] = jnp.ones_like(keep)
    keep[0:1, :TOK] = keep_ref[...].astype(F32)
    kv[...] = (flip(k_ref[...], v_ref[...]) * keep[0:1, :]).astype(BF16).reshape(HEADS, DIM, PAIR)

    qg_flat = flip(q_ref[...], g_ref[...])
    o_flat = flip(o_ref[...], o_ref[...])
    delta = jnp.sum((qg_flat * o_flat).reshape(HEADS, DIM, PAIR), axis=1)
    extra[...] = jnp.zeros_like(extra)
    extra[:, :TOK] = lse_ref[...] * (1.0 / SCALING)
    low = lax.broadcasted_iota(jnp.int32, (1, PAIR), 1) < TOK
    whole = jnp.where(low, extra[...], delta)
    first = whole.astype(BF16).astype(F32)
    second = (whole - first).astype(BF16).astype(F32)
    third = whole - first - second
    line = lax.broadcasted_iota(jnp.int32, (QROWS - DIM, PAIR), 0)
    qg[:, :DIM, :] = qg_flat.astype(BF16).reshape(HEADS, DIM, PAIR)
    for number in range(HEADS):
        rows = jnp.where(line == 0, first[number : number + 1], 0.0)
        rows = jnp.where(line == 1, second[number : number + 1], rows)
        rows = jnp.where(line == 2, third[number : number + 1], rows)
        qg[number, DIM:, :] = rows.astype(BF16)
    pl.semaphore_wait(barrier, len(partners))
    for which in (0, 1):
        arrive_own(which).start()
    for group in range(4):
        for which in (0, 1):
            for step in range(max(1, 4 * group), 4 * group + 4):
                arrive(which, step).start()

    def swap(value):
        return pltpu.roll(value, TOK, 1)

    def mix(one, two):
        return jnp.where(low, one, swap(two)), jnp.where(low, swap(one), two)

    minus = jnp.where(line < 3, -1.0, 0.0)
    fill = jnp.zeros((PAIR - QROWS, PAIR), F32)

    def lay_queries(quarter, slot):
        for pair in range(2):
            here = pl.ds(slot * QUARTER + pair * PAIR, PAIR)
            at = 4 * quarter + 2 * pair
            q, g = mix(qs[slot, at].astype(F32), qs[slot, at + 1].astype(F32))
            qt[quarter, :, here] = q[:DIM].astype(BF16)
            gt[quarter, :, here] = g[:DIM].astype(BF16)
            qa[quarter, here, :] = jnp.concatenate([q, fill], axis=0).T.astype(BF16)
            ga[quarter, here, :] = jnp.concatenate([g, fill], axis=0).T.astype(BF16)

    def lay_keys(quarter, slot):
        for pair in range(2):
            here = pl.ds(slot * QUARTER + pair * PAIR, PAIR)
            at = 4 * quarter + 2 * pair
            k, v = mix(ks[slot, at].astype(F32), ks[slot, at + 1].astype(F32))
            kt[quarter, :, here] = k.astype(BF16)
            ka[quarter, :, here] = jnp.concatenate([k, minus, fill], axis=0).astype(BF16)
            va[quarter, :, here] = jnp.concatenate([v, minus, fill], axis=0).astype(BF16)

    def ring_one(group):
        for which in (0, 1):
            for step in range(4 * group, 4 * group + 4):
                if step == 0:
                    arrive_own(which).wait()
                else:
                    arrive(which, step).wait_recv()
            ring(which, group, 0).start()
            ring(which, group, 1).start()

    def ring_two(group):
        for which in (0, 1):
            ring(which, group, 0).wait_recv()
            ring(which, group, 2).start()
            ring(which, group, 1).wait_recv()
            ring(which, group, 3).start()

    def ring_end(group):
        for which in (0, 1):
            ring(which, group, 2).wait_recv()
            ring(which, group, 3).wait_recv()

    def lay(group, slots):
        for slot in slots:
            lay_queries(group, slot)
            lay_keys(group, slot)

    def send_keys(quarter):
        for slot in range(3):
            here = pl.ds((slot + 1) * QUARTER, QUARTER)
            part_k[quarter, slot, 0] = acc_k[quarter, :, here].astype(BF16)
            part_k[quarter, slot, 1] = acc_v[quarter, :, here].astype(BF16)
            sum_keys(quarter, slot).start()

    def send_queries(quarter):
        for slot in range(3):
            here = pl.ds((slot + 1) * QUARTER, QUARTER)
            part_q[quarter, slot] = acc_q[quarter, :, here].astype(BF16)
            sum_queries(quarter, slot).start()

    def return_keys(quarter):
        for slot in range(3):
            sum_keys(quarter, slot).wait_recv()
        for pair in range(2):
            here = pl.ds(pair * PAIR, PAIR)
            k, v = acc_k[quarter, :, here], acc_v[quarter, :, here]
            for slot in range(3):
                k = k + got_k[quarter, slot, 0, :, here].astype(F32)
                v = v + got_k[quarter, slot, 1, :, here].astype(F32)
            one, two = mix(k * SCALING, v)
            at = 4 * quarter + 2 * pair
            pack_k[at] = one.astype(BF16)
            pack_k[at + 1] = two.astype(BF16)
        for step in range(4 * quarter, 4 * quarter + 4):
            leave(1, step).start()

    def return_queries(quarter):
        for slot in range(3):
            sum_queries(quarter, slot).wait_recv()
        for pair in range(2):
            here = pl.ds(pair * PAIR, PAIR)
            q = acc_q[quarter, :, here]
            for slot in range(3):
                q = q + got_q[quarter, slot, :, here].astype(F32)
            q = q * SCALING
            rest = jnp.concatenate([q[TOP:], jnp.zeros((TOP - REST, PAIR), F32)], axis=0)
            one, two = mix(q[:TOP], rest)
            at = 4 * quarter + 2 * pair
            pack_q[at] = one.astype(BF16)
            pack_q[at + 1] = two.astype(BF16)
        for step in range(4 * quarter, 4 * quarter + 4):
            leave(0, step).start()

    for ref in (acc_q, acc_k, acc_v):
        ref[...] = jnp.zeros_like(ref)
    ring_one(0)
    lay(0, (0,))
    ring_two(0)
    lay(0, (1, 2))
    ring_one(1)
    ring_end(0)
    lay(0, (3,))

    def before(turn):
        if turn == 1:
            ring_two(1)
            ring_one(2)
            lay(1, (0, 1, 2))
            ring_end(1)
            lay(1, (3,))
        if turn == 2:
            ring_two(2)
        if turn == 3:
            ring_one(3)
        if turn == 4:
            ring_end(2)
            lay(2, range(4))
        if turn == 5:
            ring_two(3)
        if turn == 9:
            ring_end(3)
            lay(3, range(4))
        if turn == 11:
            send_queries(0)
        if turn == 12:
            send_queries(1)
        if turn == 13:
            send_keys(3)
            send_queries(2)
            return_queries(0)
        if turn == 14:
            send_keys(1)
            return_queries(1)
        if turn == 15:
            send_keys(2)
            return_keys(3)
            return_queries(2)

    def score(chunk):
        query, key, rows, columns = chunk
        scores = jnp.dot(qa[query, rows, :], ka[key, :, columns], preferred_element_type=F32)
        grad_probs = jnp.dot(ga[query, rows, :], va[key, :, columns], preferred_element_type=F32)
        return scores, grad_probs

    def weigh(scores, grad_probs):
        probs = jnp.exp2(scores * (SCALING * LOG2E))
        return probs.astype(BF16), (probs * grad_probs).astype(BF16)

    def gather(chunk, probs, grad_scores):
        query, key, rows, columns = chunk
        acc_v[key, :, columns] += jnp.dot(gt[query, :, rows], probs, preferred_element_type=F32)
        acc_k[key, :, columns] += jnp.dot(qt[query, :, rows], grad_scores, preferred_element_type=F32)
        acc_q[query, :, rows] += lax.dot_general(
            kt[key, :, columns], grad_scores, (((1,), (1,)), ((), ())), preferred_element_type=F32
        )

    def tile(turn, codes):
        code_q, code_k = codes
        query, key = 3 - lax.rem(code_q, 4), lax.rem(code_k, 4)
        for at in range(1, 16):
            if at in EVENTS:
                pl.when(turn == at)(lambda at=at: before(at))
        chunks = [
            (query, key, pl.ds(at, ROWS), pl.ds(to, COLUMNS))
            for at in range(0, GROUP, ROWS)
            for to in range(0, GROUP, COLUMNS)
        ]
        ready, waiting = score(chunks[0]), None
        for number, chunk in enumerate(chunks):
            coming = score(chunks[number + 1]) if number + 1 < len(chunks) else None
            weighed = weigh(*ready)
            if waiting is not None:
                gather(chunks[number - 1], *waiting)
            waiting, ready = weighed, coming
        gather(chunks[-1], *waiting)
        return lax.div(code_q, 4), lax.div(code_k, 4)

    lax.fori_loop(0, 16, tile, (jnp.int32(QUERY_CODE), jnp.int32(KEY_CODE)))
    send_keys(0)
    send_queries(3)
    return_keys(1)
    return_keys(2)
    return_queries(3)
    return_keys(0)

    for step in range(HEADS):
        for which in (0, 1):
            if step == 0:
                leave(which, step).wait()
            else:
                leave(which, step).wait_recv()
    for step in range(1, HEADS):
        for which in (0, 1):
            arrive(which, step).wait_send()
            leave(which, step).wait_send()
    for which in (0, 1):
        for group in range(4):
            for kind in range(4):
                ring(which, group, kind).wait_send()
    for slot in range(3):
        for quarter in range(4):
            sum_queries(quarter, slot).wait_send()
            sum_keys(quarter, slot).wait_send()


def finish(back_k, back_q, keep_ref, dq_ref, dk_ref, dv_ref, keep):
    keep[:, :TOK] = jnp.broadcast_to(keep_ref[...].astype(F32), (8, TOK))
    keep[:, TOK:] = jnp.broadcast_to(keep_ref[...].astype(F32), (8, TOK))
    flat = (back_k[...].astype(F32).reshape(WIDTH, PAIR) * keep[0:1, :]).T
    dk_ref[...] = flat[:TOK].astype(BF16)
    dv_ref[...] = flat[TOK:].astype(BF16)
    pieces = []
    for number in range(HEADS):
        block = back_q[number].astype(F32)
        pieces += [block, pltpu.roll(block, TOK, 1)[:REST]]
    dq_ref[...] = jnp.concatenate(pieces, axis=0).T[:TOK].astype(BF16)


def on_device(query_vecs, key_vecs, value_vecs, attn_out, out_grad, saved_lse, kept_mask):
    shape = jax.ShapeDtypeStruct
    keep = kept_mask.reshape(1, TOK)
    dma = pltpu.SemaphoreType.DMA

    def low_bits(*dims):
        return pltpu.VMEM(dims, BF16)

    def full(*dims):
        return pltpu.VMEM(dims, F32)

    back = pl.pallas_call(
        kernel,
        out_shape=[shape((HEADS, DIM, PAIR), BF16), shape((HEADS, TOP, PAIR), BF16)],
        in_specs=[VMEM] * 7,
        out_specs=[VMEM] * 2,
        scratch_shapes=[
            full(8, PAIR),
            full(HEADS, PAIR),
            low_bits(HEADS, QROWS, PAIR),
            low_bits(HEADS, DIM, PAIR),
            low_bits(RING, HEADS, QROWS, PAIR),
            low_bits(RING, HEADS, DIM, PAIR),
            low_bits(RING, GROUP, PAIR),
            low_bits(RING, GROUP, PAIR),
            low_bits(RING, DIM, GROUP),
            low_bits(RING, DIM, GROUP),
            low_bits(RING, PAIR, GROUP),
            low_bits(RING, PAIR, GROUP),
            low_bits(RING, DIM, GROUP),
            full(RING, DIM, GROUP),
            full(RING, DIM, GROUP),
            full(RING, DIM, GROUP),
            low_bits(RING, 3, 2, DIM, QUARTER),
            low_bits(RING, 3, 2, DIM, QUARTER),
            low_bits(RING, 3, DIM, QUARTER),
            low_bits(RING, 3, DIM, QUARTER),
            low_bits(HEADS, DIM, PAIR),
            low_bits(HEADS, TOP, PAIR),
            dma((4,)),
            dma((2, HEADS)),
            dma((2, HEADS)),
            dma((2, 4, 4)),
            dma((2, 4, 4)),
            dma((4, 3)),
            dma((4, 3)),
            dma((4, 3)),
            dma((4, 3)),
            dma((2, HEADS)),
            dma((2, HEADS)),
        ],
        compiler_params=pltpu.CompilerParams(
            vmem_limit_bytes=56 * 2**20, collective_id=0, has_side_effects=True
        ),
    )(
        query_vecs, out_grad, attn_out, key_vecs, value_vecs, saved_lse.T, keep,
    )
    return pl.pallas_call(
        finish,
        out_shape=[shape((TOK, WIDTH), BF16)] * 3,
        in_specs=[VMEM] * 3,
        out_specs=[VMEM] * 3,
        scratch_shapes=[full(8, PAIR)],
    )(*back, keep)


def solution(mesh):
    queries, keys = P(("row", "col"), None), P(("col", "row"), None)
    return jax.shard_map(
        on_device,
        mesh=mesh,
        in_specs=(queries, keys, keys, queries, queries, queries, P(("col", "row"))),
        out_specs=(queries, keys, keys),
        check_vma=False,
    )
```

```python
import jax
import jax.numpy as jnp
from jax import lax
from jax.experimental import pallas as pl
from jax.experimental.pallas import tpu as pltpu
from jax.sharding import PartitionSpec as P

HEADS, DIM, TOK = 16, 80, 64
WIDTH = HEADS * DIM
RING = 4
GROUP = HEADS * TOK
PAIR = 2 * TOK
QUARTER = GROUP // RING
QROWS, TOP = 96, 48
REST = DIM - TOP
SCALING = DIM**-0.5
LOG2E = 1.4426950408889634
MESH = pl.DeviceIdType.MESH
F32, BF16 = jnp.float32, jnp.bfloat16
STEPS = (0, 1, -1, 2, -2, 3, -3, 4, -4, 5, -5, 6, -6, 7, -7, 8)
ROWS, COLUMNS = 256, 512
ORDER = (
    (0, 0), (0, 1), (1, 0), (1, 1), (0, 2), (1, 2), (2, 0), (2, 1), (2, 2),
    (3, 0), (3, 1), (3, 2), (3, 3), (0, 3), (1, 3), (2, 3),
)
QUERY_CODE = sum((3 - q) * 4**turn for turn, (q, _) in enumerate(ORDER))
KEY_CODE = sum((3 - k) * 4**turn for turn, (_, k) in enumerate(ORDER))
EVENTS = (1, 2, 3, 4, 5, 9, 10, 11, 12, 13, 14, 15)
VMEM = pl.BlockSpec(memory_space=pltpu.VMEM)


def kernel(
    q_any, g_any, o_any, k_any, v_any, lse_ref, keep_ref, back_k, back_q,
    q_ref, g_ref, o_ref, k_ref, v_ref,
    keep, extra, qg, kv, qs, ks, qa, ga, qt, gt, ka, va, acc_q, acc_k, acc_v,
    part_k, got_k, part_q, got_q, pack_k, pack_q,
    load_sem, local_sem, in_send, in_recv, ring_send, ring_recv,
    sum_send, sum_recv, sumq_send, sumq_recv, out_send, out_recv,
):
    row, col = lax.axis_index("row"), lax.axis_index("col")
    high = lax.rem(col, 2)
    head = high * 8 + row
    x, y = lax.rem(lax.div(col, 2), RING), lax.div(col, 2 * RING)

    def head_device(step):
        other = lax.rem(head + step + HEADS, HEADS)
        return other, (lax.rem(other, 8), col - high + lax.div(other, 8))

    def side_device(which, step):
        if which == 0:
            return (row, col + 2 * (lax.rem(x + step + RING, RING) - x))
        return (row, col + 2 * RING * (lax.rem(y + step + RING, RING) - y))

    def remote(source, target, send, recv, device):
        return pltpu.make_async_remote_copy(
            src_ref=source, dst_ref=target, send_sem=send, recv_sem=recv,
            device_id=device, device_id_type=MESH,
        )

    def arrive(which, step):
        other, device = head_device(STEPS[step])
        source, target = ((qg, qs), (kv, ks))[which]
        return remote(
            source.at[other], target.at[0, step],
            in_send.at[which, step], in_recv.at[which, step], device,
        )

    def arrive_own(which):
        source, target = ((qg, qs), (kv, ks))[which]
        return pltpu.make_async_copy(source.at[head], target.at[0, 0], local_sem.at[which])

    def ring(which, group, kind):
        ref = (qs, ks)[which]
        source, target, first, count, step = (
            (0, 1, 0, 4, 1), (0, 2, 0, 4, -1), (1, 3, 0, 2, 1), (2, 3, 2, 2, -1),
        )[kind]
        part = pl.ds(4 * group + first, count)
        return remote(
            ref.at[source, part], ref.at[target, part],
            ring_send.at[which, group, kind], ring_recv.at[which, group, kind],
            side_device(which, step),
        )

    back_steps = (-1, 1, 2)

    def sum_keys(quarter, slot):
        return remote(
            part_k.at[quarter, slot], got_k.at[quarter, slot],
            sum_send.at[quarter, slot], sum_recv.at[quarter, slot],
            side_device(1, back_steps[slot]),
        )

    def sum_queries(quarter, slot):
        return remote(
            part_q.at[quarter, slot], got_q.at[quarter, slot],
            sumq_send.at[quarter, slot], sumq_recv.at[quarter, slot],
            side_device(0, back_steps[slot]),
        )

    def leave(which, step):
        source, target = ((pack_q, back_q), (pack_k, back_k))[which]
        if step == 0:
            return pltpu.make_async_copy(source.at[0], target.at[head], local_sem.at[2 + which])
        _, device = head_device(-STEPS[step])
        return remote(
            source.at[step], target.at[head],
            out_send.at[which, step], out_recv.at[which, step], device,
        )

    barrier = pltpu.get_barrier_semaphore()
    partners = [head_device(step)[1] for step in range(1, HEADS)]
    partners += [side_device(which, step) for which in (0, 1) for step in back_steps]
    for device in partners:
        pl.semaphore_signal(barrier, inc=1, device_id=device, device_id_type=MESH)

    loads = [
        pltpu.make_async_copy(source, target, load_sem.at[number])
        for number, (source, target) in enumerate(
            ((k_any, k_ref), (v_any, v_ref), (q_any, q_ref), (g_any, g_ref), (o_any, o_ref))
        )
    ]
    for load in loads:
        load.start()

    def flip(top, bottom):
        return jnp.concatenate([top, bottom], axis=0).astype(F32).T

    loads[0].wait()
    loads[1].wait()
    keep[...] = jnp.ones_like(keep)
    keep[0:1, :TOK] = keep_ref[...].astype(F32)
    kv[...] = (flip(k_ref[...], v_ref[...]) * keep[0:1, :]).astype(BF16).reshape(HEADS, DIM, PAIR)

    for load in loads[2:]:
        load.wait()
    qg_flat = flip(q_ref[...], g_ref[...])
    o_flat = flip(o_ref[...], o_ref[...])
    delta = jnp.sum((qg_flat * o_flat).reshape(HEADS, DIM, PAIR), axis=1)
    extra[...] = jnp.zeros_like(extra)
    extra[:, :TOK] = lse_ref[...] * (1.0 / SCALING)
    low = lax.broadcasted_iota(jnp.int32, (1, PAIR), 1) < TOK
    whole = jnp.where(low, extra[...], delta)
    first = whole.astype(BF16).astype(F32)
    second = (whole - first).astype(BF16).astype(F32)
    third = whole - first - second
    line = lax.broadcasted_iota(jnp.int32, (QROWS - DIM, PAIR), 0)
    qg[:, :DIM, :] = qg_flat.astype(BF16).reshape(HEADS, DIM, PAIR)
    for number in range(HEADS):
        rows = jnp.where(line == 0, first[number : number + 1], 0.0)
        rows = jnp.where(line == 1, second[number : number + 1], rows)
        rows = jnp.where(line == 2, third[number : number + 1], rows)
        qg[number, DIM:, :] = rows.astype(BF16)
    pl.semaphore_wait(barrier, len(partners))
    for which in (0, 1):
        arrive_own(which).start()
    for group in range(4):
        for which in (0, 1):
            for step in range(max(1, 4 * group), 4 * group + 4):
                arrive(which, step).start()

    def swap(value):
        return pltpu.roll(value, TOK, 1)

    def mix(one, two):
        return jnp.where(low, one, swap(two)), jnp.where(low, swap(one), two)

    minus = jnp.where(line < 3, -1.0, 0.0)
    fill = jnp.zeros((PAIR - QROWS, PAIR), F32)

    def lay_queries(quarter, slot):
        for pair in range(2):
            here = pl.ds(slot * QUARTER + pair * PAIR, PAIR)
            at = 4 * quarter + 2 * pair
            q, g = mix(qs[slot, at].astype(F32), qs[slot, at + 1].astype(F32))
            qt[quarter, :, here] = q[:DIM].astype(BF16)
            gt[quarter, :, here] = g[:DIM].astype(BF16)
            qa[quarter, here, :] = jnp.concatenate([q, fill], axis=0).T.astype(BF16)
            ga[quarter, here, :] = jnp.concatenate([g, fill], axis=0).T.astype(BF16)

    def lay_keys(quarter, slot):
        for pair in range(2):
            here = pl.ds(slot * QUARTER + pair * PAIR, PAIR)
            at = 4 * quarter + 2 * pair
            k, v = mix(ks[slot, at].astype(F32), ks[slot, at + 1].astype(F32))
            ka[quarter, :, here] = jnp.concatenate([k, minus, fill], axis=0).astype(BF16)
            va[quarter, :, here] = jnp.concatenate([v, minus, fill], axis=0).astype(BF16)

    def ring_one(group):
        for which in (0, 1):
            for step in range(4 * group, 4 * group + 4):
                if step == 0:
                    arrive_own(which).wait()
                else:
                    arrive(which, step).wait_recv()
            ring(which, group, 0).start()
            ring(which, group, 1).start()

    def ring_two(group):
        for which in (0, 1):
            ring(which, group, 0).wait_recv()
            ring(which, group, 2).start()
            ring(which, group, 1).wait_recv()
            ring(which, group, 3).start()

    def ring_end(group):
        for which in (0, 1):
            ring(which, group, 2).wait_recv()
            ring(which, group, 3).wait_recv()

    def lay(group, slots):
        for slot in slots:
            lay_queries(group, slot)
            lay_keys(group, slot)

    def send_keys(quarter):
        for slot in (2, 0, 1):
            here = pl.ds((slot + 1) * QUARTER, QUARTER)
            part_k[quarter, slot, 0] = acc_k[quarter, :, here].astype(BF16)
            part_k[quarter, slot, 1] = acc_v[quarter, :, here].astype(BF16)
            sum_keys(quarter, slot).start()

    def send_queries(quarter):
        for slot in (2, 0, 1):
            here = pl.ds((slot + 1) * QUARTER, QUARTER)
            part_q[quarter, slot] = acc_q[quarter, :, here].astype(BF16)
            sum_queries(quarter, slot).start()

    def return_keys(quarter):
        for slot in range(3):
            sum_keys(quarter, slot).wait_recv()
        for pair in range(2):
            here = pl.ds(pair * PAIR, PAIR)
            k, v = acc_k[quarter, :, here], acc_v[quarter, :, here]
            for slot in range(3):
                k = k + got_k[quarter, slot, 0, :, here].astype(F32)
                v = v + got_k[quarter, slot, 1, :, here].astype(F32)
            one, two = mix(k * SCALING, v)
            at = 4 * quarter + 2 * pair
            pack_k[at] = one.astype(BF16)
            pack_k[at + 1] = two.astype(BF16)
        for step in range(4 * quarter, 4 * quarter + 4):
            leave(1, step).start()

    def return_queries(quarter):
        for slot in range(3):
            sum_queries(quarter, slot).wait_recv()
        for pair in range(2):
            here = pl.ds(pair * PAIR, PAIR)
            q = acc_q[quarter, :, here]
            for slot in range(3):
                q = q + got_q[quarter, slot, :, here].astype(F32)
            q = q * SCALING
            rest = jnp.concatenate([q[TOP:], jnp.zeros((TOP - REST, PAIR), F32)], axis=0)
            one, two = mix(q[:TOP], rest)
            at = 4 * quarter + 2 * pair
            pack_q[at] = one.astype(BF16)
            pack_q[at + 1] = two.astype(BF16)
        for step in range(4 * quarter, 4 * quarter + 4):
            leave(0, step).start()

    for ref in (acc_q, acc_k, acc_v):
        ref[...] = jnp.zeros_like(ref)
    ring_one(0)
    lay(0, (0,))
    ring_two(0)
    ring_one(1)
    lay(0, (1, 2))
    ring_end(0)
    lay(0, (3,))
    ring_two(1)

    def before(turn):
        if turn == 1:
            ring_one(2)
            ring_end(1)
            lay(1, range(4))
        if turn == 2:
            ring_two(2)
        if turn == 3:
            ring_one(3)
        if turn == 4:
            ring_end(2)
            lay(2, range(4))
        if turn == 5:
            ring_two(3)
        if turn == 9:
            ring_end(3)
            lay(3, range(4))
        if turn == 10:
            send_keys(0)
        if turn == 11:
            send_keys(1)
        if turn == 12:
            send_keys(2)
            return_keys(0)
        if turn == 13:
            send_queries(3)
        if turn == 14:
            send_queries(0)
            return_keys(1)
        if turn == 15:
            send_queries(1)
            return_queries(3)

    def score(chunk):
        query, key, rows, columns = chunk
        scores = jnp.dot(qa[query, rows, :], ka[key, :, columns], preferred_element_type=F32)
        grad_probs = jnp.dot(ga[query, rows, :], va[key, :, columns], preferred_element_type=F32)
        return scores, grad_probs

    def weigh(scores, grad_probs):
        probs = jnp.exp2(scores * (SCALING * LOG2E))
        return probs.astype(BF16), (probs * grad_probs).astype(BF16)

    def gather(chunk, probs, grad_scores):
        query, key, rows, columns = chunk
        acc_v[key, :, columns] += jnp.dot(gt[query, :, rows], probs, preferred_element_type=F32)
        acc_k[key, :, columns] += jnp.dot(qt[query, :, rows], grad_scores, preferred_element_type=F32)
        acc_q[query, :, rows] += lax.dot_general(
            ka[key, :DIM, columns], grad_scores, (((1,), (1,)), ((), ())), preferred_element_type=F32
        )

    def tile(turn, codes):
        code_q, code_k = codes
        query, key = 3 - lax.rem(code_q, 4), 3 - lax.rem(code_k, 4)
        for at in range(1, 16):
            if at in EVENTS:
                pl.when(turn == at)(lambda at=at: before(at))
        chunks = [
            (query, key, pl.ds(at, ROWS), pl.ds(to, COLUMNS))
            for at in range(0, GROUP, ROWS)
            for to in range(0, GROUP, COLUMNS)
        ]
        ready, waiting = score(chunks[0]), None
        for number, chunk in enumerate(chunks):
            coming = score(chunks[number + 1]) if number + 1 < len(chunks) else None
            weighed = weigh(*ready)
            if waiting is not None:
                gather(chunks[number - 1], *waiting)
            waiting, ready = weighed, coming
        gather(chunks[-1], *waiting)
        return lax.div(code_q, 4), lax.div(code_k, 4)

    lax.fori_loop(0, 16, tile, (jnp.int32(QUERY_CODE), jnp.int32(KEY_CODE)))
    send_keys(3)
    send_queries(2)
    return_keys(2)
    return_queries(0)
    return_queries(1)
    return_queries(2)
    return_keys(3)

    for step in range(HEADS):
        for which in (0, 1):
            if step == 0:
                leave(which, step).wait()
            else:
                leave(which, step).wait_recv()
    for step in range(1, HEADS):
        for which in (0, 1):
            arrive(which, step).wait_send()
            leave(which, step).wait_send()
    for which in (0, 1):
        for group in range(4):
            for kind in range(4):
                ring(which, group, kind).wait_send()
    for slot in range(3):
        for quarter in range(4):
            sum_queries(quarter, slot).wait_send()
            sum_keys(quarter, slot).wait_send()


def finish(back_k, back_q, keep_ref, dq_ref, dk_ref, dv_ref, keep):
    keep[:, :TOK] = jnp.broadcast_to(keep_ref[...].astype(F32), (8, TOK))
    keep[:, TOK:] = jnp.broadcast_to(keep_ref[...].astype(F32), (8, TOK))
    flat = (back_k[...].astype(F32).reshape(WIDTH, PAIR) * keep[0:1, :]).T
    dk_ref[...] = flat[:TOK].astype(BF16)
    dv_ref[...] = flat[TOK:].astype(BF16)
    pieces = []
    for number in range(HEADS):
        block = back_q[number].astype(F32)
        pieces += [block, pltpu.roll(block, TOK, 1)[:REST]]
    dq_ref[...] = jnp.concatenate(pieces, axis=0).T[:TOK].astype(BF16)


def on_device(query_vecs, key_vecs, value_vecs, attn_out, out_grad, saved_lse, kept_mask):
    shape = jax.ShapeDtypeStruct
    keep = kept_mask.reshape(1, TOK)
    dma = pltpu.SemaphoreType.DMA

    def low_bits(*dims):
        return pltpu.VMEM(dims, BF16)

    def full(*dims):
        return pltpu.VMEM(dims, F32)

    back = pl.pallas_call(
        kernel,
        out_shape=[shape((HEADS, DIM, PAIR), BF16), shape((HEADS, TOP, PAIR), BF16)],
        in_specs=[pl.BlockSpec(memory_space=pl.ANY)] * 5 + [VMEM] * 2,
        out_specs=[VMEM] * 2,
        scratch_shapes=[
            *[low_bits(TOK, WIDTH)] * 5,
            full(8, PAIR),
            full(HEADS, PAIR),
            low_bits(HEADS, QROWS, PAIR),
            low_bits(HEADS, DIM, PAIR),
            low_bits(RING, HEADS, QROWS, PAIR),
            low_bits(RING, HEADS, DIM, PAIR),
            low_bits(RING, GROUP, PAIR),
            low_bits(RING, GROUP, PAIR),
            low_bits(RING, DIM, GROUP),
            low_bits(RING, DIM, GROUP),
            low_bits(RING, PAIR, GROUP),
            low_bits(RING, PAIR, GROUP),
            full(RING, DIM, GROUP),
            full(RING, DIM, GROUP),
            full(RING, DIM, GROUP),
            low_bits(RING, 3, 2, DIM, QUARTER),
            low_bits(RING, 3, 2, DIM, QUARTER),
            low_bits(RING, 3, DIM, QUARTER),
            low_bits(RING, 3, DIM, QUARTER),
            low_bits(HEADS, DIM, PAIR),
            low_bits(HEADS, TOP, PAIR),
            dma((5,)),
            dma((4,)),
            dma((2, HEADS)),
            dma((2, HEADS)),
            dma((2, 4, 4)),
            dma((2, 4, 4)),
            dma((4, 3)),
            dma((4, 3)),
            dma((4, 3)),
            dma((4, 3)),
            dma((2, HEADS)),
            dma((2, HEADS)),
        ],
        compiler_params=pltpu.CompilerParams(
            vmem_limit_bytes=56 * 2**20, collective_id=0, has_side_effects=True
        ),
    )(
        query_vecs, out_grad, attn_out, key_vecs, value_vecs, saved_lse.T, keep,
    )
    return pl.pallas_call(
        finish,
        out_shape=[shape((TOK, WIDTH), BF16)] * 3,
        in_specs=[VMEM] * 3,
        out_specs=[VMEM] * 3,
        scratch_shapes=[full(8, PAIR)],
    )(*back, keep)


def solution(mesh):
    queries, keys = P(("row", "col"), None), P(("col", "row"), None)
    return jax.shard_map(
        on_device,
        mesh=mesh,
        in_specs=(queries, keys, keys, queries, queries, queries, P(("col", "row"))),
        out_specs=(queries, keys, keys),
        check_vma=False,
    )
```

```python
import jax
import jax.numpy as jnp
from jax import lax
from jax.experimental import pallas as pl
from jax.experimental.pallas import tpu as pltpu
from jax.sharding import PartitionSpec as P

HEADS, DIM, TOK = 16, 80, 64
WIDTH = HEADS * DIM
RING = 4
GROUP = HEADS * TOK
PAIR = 2 * TOK
QUARTER = GROUP // RING
QROWS, TOP = 96, 48
REST = DIM - TOP
SCALING = DIM**-0.5
LOG2E = 1.4426950408889634
MESH = pl.DeviceIdType.MESH
F32, BF16 = jnp.float32, jnp.bfloat16
STEPS = (0, 1, -1, 2, -2, 3, -3, 4, -4, 5, -5, 6, -6, 7, -7, 8)
ROWS, COLUMNS = 256, 512
ORDER = (
    (0, 0), (0, 1), (1, 0), (1, 1), (0, 2), (1, 2), (2, 0), (2, 1), (2, 2),
    (3, 0), (3, 1), (3, 2), (3, 3), (0, 3), (1, 3), (2, 3),
)
QUERY_CODE = sum((3 - q) * 4**turn for turn, (q, _) in enumerate(ORDER))
KEY_CODE = sum((3 - k) * 4**turn for turn, (_, k) in enumerate(ORDER))
EARLY, LATE = (1, 2, 3, 4, 5), (9, 10, 11, 12, 13, 14, 15)
VMEM = pl.BlockSpec(memory_space=pltpu.VMEM)


def kernel(
    q_any, g_any, o_any, k_any, v_any, lse_ref, keep_ref, back_k, back_q,
    q_ref, g_ref, o_ref, k_ref, v_ref,
    keep, extra, qg, kv, qs, ks, qa, ga, qt, gt, ka, va, acc_q, acc_k, acc_v,
    part_k, got_k, part_q, got_q, pack_k, pack_q,
    load_sem, local_sem, in_send, in_recv, ring_send, ring_recv,
    sum_send, sum_recv, sumq_send, sumq_recv, out_send, out_recv,
):
    row, col = lax.axis_index("row"), lax.axis_index("col")
    high = lax.rem(col, 2)
    head = high * 8 + row
    x, y = lax.rem(lax.div(col, 2), RING), lax.div(col, 2 * RING)

    def head_device(step):
        other = lax.rem(head + step + HEADS, HEADS)
        return other, (lax.rem(other, 8), col - high + lax.div(other, 8))

    def side_device(which, step):
        if which == 0:
            return (row, col + 2 * (lax.rem(x + step + RING, RING) - x))
        return (row, col + 2 * RING * (lax.rem(y + step + RING, RING) - y))

    def remote(source, target, send, recv, device):
        return pltpu.make_async_remote_copy(
            src_ref=source, dst_ref=target, send_sem=send, recv_sem=recv,
            device_id=device, device_id_type=MESH,
        )

    def arrive(which, step):
        other, device = head_device(STEPS[step])
        source, target = ((qg, qs), (kv, ks))[which]
        return remote(
            source.at[other], target.at[0, step],
            in_send.at[which, step], in_recv.at[which, step], device,
        )

    def arrive_own(which):
        source, target = ((qg, qs), (kv, ks))[which]
        return pltpu.make_async_copy(source.at[head], target.at[0, 0], local_sem.at[which])

    def ring(which, group, kind):
        ref = (qs, ks)[which]
        source, target, first, count, step = (
            (0, 1, 0, 4, 1), (0, 2, 0, 4, -1), (1, 3, 0, 2, 1), (2, 3, 2, 2, -1),
        )[kind]
        part = pl.ds(4 * group + first, count)
        return remote(
            ref.at[source, part], ref.at[target, part],
            ring_send.at[which, group, kind], ring_recv.at[which, group, kind],
            side_device(which, step),
        )

    back_steps = (-1, 1, 2)

    def sum_keys(quarter, slot):
        return remote(
            part_k.at[quarter, slot], got_k.at[quarter, slot],
            sum_send.at[quarter, slot], sum_recv.at[quarter, slot],
            side_device(1, back_steps[slot]),
        )

    def sum_queries(quarter, slot):
        return remote(
            part_q.at[quarter, slot], got_q.at[quarter, slot],
            sumq_send.at[quarter, slot], sumq_recv.at[quarter, slot],
            side_device(0, back_steps[slot]),
        )

    def leave(which, step):
        source, target = ((pack_q, back_q), (pack_k, back_k))[which]
        if step == 0:
            return pltpu.make_async_copy(source.at[0], target.at[head], local_sem.at[2 + which])
        _, device = head_device(-STEPS[step])
        return remote(
            source.at[step], target.at[head],
            out_send.at[which, step], out_recv.at[which, step], device,
        )

    barrier = pltpu.get_barrier_semaphore()
    partners = [head_device(step)[1] for step in range(1, HEADS)]
    partners += [side_device(which, step) for which in (0, 1) for step in back_steps]
    for device in partners:
        pl.semaphore_signal(barrier, inc=1, device_id=device, device_id_type=MESH)

    loads = [
        pltpu.make_async_copy(source, target, load_sem.at[number])
        for number, (source, target) in enumerate(
            ((k_any, k_ref), (v_any, v_ref), (q_any, q_ref), (g_any, g_ref), (o_any, o_ref))
        )
    ]
    for load in loads:
        load.start()

    def flip(top, bottom):
        return jnp.concatenate([top, bottom], axis=0).astype(F32).T

    loads[0].wait()
    loads[1].wait()
    keep[...] = jnp.ones_like(keep)
    keep[0:1, :TOK] = keep_ref[...].astype(F32)
    kv[...] = (flip(k_ref[...], v_ref[...]) * keep[0:1, :]).astype(BF16).reshape(HEADS, DIM, PAIR)

    for load in loads[2:]:
        load.wait()
    qg_flat = flip(q_ref[...], g_ref[...])
    o_flat = flip(o_ref[...], o_ref[...])
    delta = jnp.sum((qg_flat * o_flat).reshape(HEADS, DIM, PAIR), axis=1)
    extra[...] = jnp.zeros_like(extra)
    extra[:, :TOK] = lse_ref[...] * (1.0 / SCALING)
    low = lax.broadcasted_iota(jnp.int32, (1, PAIR), 1) < TOK
    whole = jnp.where(low, extra[...], delta)
    first = whole.astype(BF16).astype(F32)
    second = (whole - first).astype(BF16).astype(F32)
    third = whole - first - second
    line = lax.broadcasted_iota(jnp.int32, (QROWS - DIM, PAIR), 0)
    qg[:, :DIM, :] = qg_flat.astype(BF16).reshape(HEADS, DIM, PAIR)
    for number in range(HEADS):
        rows = jnp.where(line == 0, first[number : number + 1], 0.0)
        rows = jnp.where(line == 1, second[number : number + 1], rows)
        rows = jnp.where(line == 2, third[number : number + 1], rows)
        qg[number, DIM:, :] = rows.astype(BF16)
    pl.semaphore_wait(barrier, len(partners))
    for which in (0, 1):
        arrive_own(which).start()
    for group in range(4):
        for which in (0, 1):
            for step in range(max(1, 4 * group), 4 * group + 4):
                arrive(which, step).start()

    def swap(value):
        return pltpu.roll(value, TOK, 1)

    def mix(one, two):
        return jnp.where(low, one, swap(two)), jnp.where(low, swap(one), two)

    minus = jnp.where(line < 3, -1.0, 0.0)
    fill = jnp.zeros((PAIR - QROWS, PAIR), F32)

    def lay_queries(quarter, slot):
        for pair in range(2):
            here = pl.ds(slot * QUARTER + pair * PAIR, PAIR)
            at = 4 * quarter + 2 * pair
            q, g = mix(qs[slot, at].astype(F32), qs[slot, at + 1].astype(F32))
            qt[quarter, :, here] = q[:DIM].astype(BF16)
            gt[quarter, :, here] = g[:DIM].astype(BF16)
            qa[quarter, here, :] = jnp.concatenate([q, fill], axis=0).T.astype(BF16)
            ga[quarter, here, :] = jnp.concatenate([g, fill], axis=0).T.astype(BF16)

    def lay_keys(quarter, slot):
        for pair in range(2):
            here = pl.ds(slot * QUARTER + pair * PAIR, PAIR)
            at = 4 * quarter + 2 * pair
            k, v = mix(ks[slot, at].astype(F32), ks[slot, at + 1].astype(F32))
            ka[quarter, :, here] = jnp.concatenate([k, minus, fill], axis=0).astype(BF16)
            va[quarter, :, here] = jnp.concatenate([v, minus, fill], axis=0).astype(BF16)

    def ring_one(group):
        for which in (0, 1):
            for step in range(4 * group, 4 * group + 4):
                if step == 0:
                    arrive_own(which).wait()
                else:
                    arrive(which, step).wait_recv()
            ring(which, group, 0).start()
            ring(which, group, 1).start()

    def ring_two(group):
        for which in (0, 1):
            ring(which, group, 0).wait_recv()
            ring(which, group, 2).start()
            ring(which, group, 1).wait_recv()
            ring(which, group, 3).start()

    def ring_end(group):
        for which in (0, 1):
            ring(which, group, 2).wait_recv()
            ring(which, group, 3).wait_recv()

    def lay(group, slots):
        for slot in slots:
            lay_queries(group, slot)
            lay_keys(group, slot)

    def send_keys(quarter):
        for slot in (2, 0, 1):
            here = pl.ds((slot + 1) * QUARTER, QUARTER)
            part_k[quarter, slot, 0] = acc_k[quarter, :, here].astype(BF16)
            part_k[quarter, slot, 1] = acc_v[quarter, :, here].astype(BF16)
            sum_keys(quarter, slot).start()

    def send_queries(quarter):
        for slot in (2, 0, 1):
            here = pl.ds((slot + 1) * QUARTER, QUARTER)
            part_q[quarter, slot] = acc_q[quarter, :, here].astype(BF16)
            sum_queries(quarter, slot).start()

    def return_keys(quarter):
        for slot in range(3):
            sum_keys(quarter, slot).wait_recv()
        for pair in range(2):
            here = pl.ds(pair * PAIR, PAIR)
            k, v = acc_k[quarter, :, here], acc_v[quarter, :, here]
            for slot in range(3):
                k = k + got_k[quarter, slot, 0, :, here].astype(F32)
                v = v + got_k[quarter, slot, 1, :, here].astype(F32)
            one, two = mix(k * SCALING, v)
            at = 4 * quarter + 2 * pair
            pack_k[at] = one.astype(BF16)
            pack_k[at + 1] = two.astype(BF16)
        for step in range(4 * quarter, 4 * quarter + 4):
            leave(1, step).start()

    def return_queries(quarter):
        for slot in range(3):
            sum_queries(quarter, slot).wait_recv()
        for pair in range(2):
            here = pl.ds(pair * PAIR, PAIR)
            q = acc_q[quarter, :, here]
            for slot in range(3):
                q = q + got_q[quarter, slot, :, here].astype(F32)
            q = q * SCALING
            rest = jnp.concatenate([q[TOP:], jnp.zeros((TOP - REST, PAIR), F32)], axis=0)
            one, two = mix(q[:TOP], rest)
            at = 4 * quarter + 2 * pair
            pack_q[at] = one.astype(BF16)
            pack_q[at + 1] = two.astype(BF16)
        for step in range(4 * quarter, 4 * quarter + 4):
            leave(0, step).start()

    for ref in (acc_q, acc_k, acc_v):
        ref[...] = jnp.zeros_like(ref)
    ring_one(0)
    lay(0, (0,))
    ring_two(0)
    ring_one(1)
    lay(0, (1, 2))
    ring_end(0)
    lay(0, (3,))
    ring_two(1)

    def before(turn):
        if turn == 1:
            ring_one(2)
            ring_end(1)
            lay(1, range(4))
        if turn == 2:
            ring_two(2)
        if turn == 3:
            ring_one(3)
        if turn == 4:
            ring_end(2)
            lay(2, range(4))
        if turn == 5:
            ring_two(3)
        if turn == 9:
            ring_end(3)
            lay(3, range(4))
        if turn == 10:
            send_keys(0)
        if turn == 11:
            send_keys(1)
        if turn == 12:
            send_keys(2)
            return_keys(0)
        if turn == 13:
            send_queries(3)
        if turn == 14:
            send_queries(0)
            return_keys(1)
        if turn == 15:
            send_queries(1)
            return_queries(3)

    def score(chunk):
        query, key, rows, columns = chunk
        scores = jnp.dot(qa[query, rows, :], ka[key, :, columns], preferred_element_type=F32)
        grad_probs = jnp.dot(ga[query, rows, :], va[key, :, columns], preferred_element_type=F32)
        return scores, grad_probs

    def weigh(scores, grad_probs):
        probs = jnp.exp2(scores * (SCALING * LOG2E))
        return probs.astype(BF16), (probs * grad_probs).astype(BF16)

    def gather(chunk, probs, grad_scores):
        query, key, rows, columns = chunk
        acc_v[key, :, columns] += jnp.dot(gt[query, :, rows], probs, preferred_element_type=F32)
        acc_k[key, :, columns] += jnp.dot(qt[query, :, rows], grad_scores, preferred_element_type=F32)
        acc_q[query, :, rows] += lax.dot_general(
            ka[key, :DIM, columns], grad_scores, (((1,), (1,)), ((), ())), preferred_element_type=F32
        )

    def tile(turn, codes):
        code_q, code_k = codes
        query, key = 3 - lax.rem(code_q, 4), 3 - lax.rem(code_k, 4)

        @pl.when(turn < 6)
        def _():
            for at in EARLY:
                pl.when(turn == at)(lambda at=at: before(at))

        @pl.when(turn > 8)
        def _():
            for at in LATE:
                pl.when(turn == at)(lambda at=at: before(at))

        chunks = [
            (query, key, pl.ds(at, ROWS), pl.ds(to, COLUMNS))
            for at in range(0, GROUP, ROWS)
            for to in range(0, GROUP, COLUMNS)
        ]
        ready, waiting = score(chunks[0]), None
        for number, chunk in enumerate(chunks):
            coming = score(chunks[number + 1]) if number + 1 < len(chunks) else None
            weighed = weigh(*ready)
            if waiting is not None:
                gather(chunks[number - 1], *waiting)
            waiting, ready = weighed, coming
        gather(chunks[-1], *waiting)
        return lax.div(code_q, 4), lax.div(code_k, 4)

    lax.fori_loop(0, 16, tile, (jnp.int32(QUERY_CODE), jnp.int32(KEY_CODE)))
    send_keys(3)
    send_queries(2)
    return_keys(2)
    return_queries(0)
    return_queries(1)
    return_queries(2)
    return_keys(3)

    for step in range(HEADS):
        for which in (0, 1):
            if step == 0:
                leave(which, step).wait()
            else:
                leave(which, step).wait_recv()
    for step in range(1, HEADS):
        for which in (0, 1):
            arrive(which, step).wait_send()
            leave(which, step).wait_send()
    for which in (0, 1):
        for group in range(4):
            for kind in range(4):
                ring(which, group, kind).wait_send()
    for slot in range(3):
        for quarter in range(4):
            sum_queries(quarter, slot).wait_send()
            sum_keys(quarter, slot).wait_send()


def finish(back_k, back_q, keep_ref, dq_ref, dk_ref, dv_ref, keep):
    keep[:, :TOK] = jnp.broadcast_to(keep_ref[...].astype(F32), (8, TOK))
    keep[:, TOK:] = jnp.broadcast_to(keep_ref[...].astype(F32), (8, TOK))
    flat = (back_k[...].astype(F32).reshape(WIDTH, PAIR) * keep[0:1, :]).T
    dk_ref[...] = flat[:TOK].astype(BF16)
    dv_ref[...] = flat[TOK:].astype(BF16)
    pieces = []
    for number in range(HEADS):
        block = back_q[number].astype(F32)
        pieces += [block, pltpu.roll(block, TOK, 1)[:REST]]
    dq_ref[...] = jnp.concatenate(pieces, axis=0).T[:TOK].astype(BF16)


def on_device(query_vecs, key_vecs, value_vecs, attn_out, out_grad, saved_lse, kept_mask):
    shape = jax.ShapeDtypeStruct
    keep = kept_mask.reshape(1, TOK)
    dma = pltpu.SemaphoreType.DMA

    def low_bits(*dims):
        return pltpu.VMEM(dims, BF16)

    def full(*dims):
        return pltpu.VMEM(dims, F32)

    back = pl.pallas_call(
        kernel,
        out_shape=[shape((HEADS, DIM, PAIR), BF16), shape((HEADS, TOP, PAIR), BF16)],
        in_specs=[pl.BlockSpec(memory_space=pl.ANY)] * 5 + [VMEM] * 2,
        out_specs=[VMEM] * 2,
        scratch_shapes=[
            *[low_bits(TOK, WIDTH)] * 5,
            full(8, PAIR),
            full(HEADS, PAIR),
            low_bits(HEADS, QROWS, PAIR),
            low_bits(HEADS, DIM, PAIR),
            low_bits(RING, HEADS, QROWS, PAIR),
            low_bits(RING, HEADS, DIM, PAIR),
            low_bits(RING, GROUP, PAIR),
            low_bits(RING, GROUP, PAIR),
            low_bits(RING, DIM, GROUP),
            low_bits(RING, DIM, GROUP),
            low_bits(RING, PAIR, GROUP),
            low_bits(RING, PAIR, GROUP),
            full(RING, DIM, GROUP),
            full(RING, DIM, GROUP),
            full(RING, DIM, GROUP),
            low_bits(RING, 3, 2, DIM, QUARTER),
            low_bits(RING, 3, 2, DIM, QUARTER),
            low_bits(RING, 3, DIM, QUARTER),
            low_bits(RING, 3, DIM, QUARTER),
            low_bits(HEADS, DIM, PAIR),
            low_bits(HEADS, TOP, PAIR),
            dma((5,)),
            dma((4,)),
            dma((2, HEADS)),
            dma((2, HEADS)),
            dma((2, 4, 4)),
            dma((2, 4, 4)),
            dma((4, 3)),
            dma((4, 3)),
            dma((4, 3)),
            dma((4, 3)),
            dma((2, HEADS)),
            dma((2, HEADS)),
        ],
        compiler_params=pltpu.CompilerParams(
            vmem_limit_bytes=56 * 2**20, collective_id=0, has_side_effects=True
        ),
    )(
        query_vecs, out_grad, attn_out, key_vecs, value_vecs, saved_lse.T, keep,
    )
    return pl.pallas_call(
        finish,
        out_shape=[shape((TOK, WIDTH), BF16)] * 3,
        in_specs=[VMEM] * 3,
        out_specs=[VMEM] * 3,
        scratch_shapes=[full(8, PAIR)],
    )(*back, keep)


def solution(mesh):
    queries, keys = P(("row", "col"), None), P(("col", "row"), None)
    return jax.shard_map(
        on_device,
        mesh=mesh,
        in_specs=(queries, keys, keys, queries, queries, queries, P(("col", "row"))),
        out_specs=(queries, keys, keys),
        check_vma=False,
    )
```

```python
import jax
import jax.numpy as jnp
from jax import lax
from jax.experimental import pallas as pl
from jax.experimental.pallas import tpu as pltpu
from jax.sharding import PartitionSpec as P

HEADS, DIM, TOK = 16, 80, 64
WIDTH = HEADS * DIM
RING = 4
GROUP = HEADS * TOK
PAIR = 2 * TOK
QUARTER = GROUP // RING
QROWS, TOP = 96, 48
REST = DIM - TOP
SCALING = DIM**-0.5
LOG2E = 1.4426950408889634
MESH = pl.DeviceIdType.MESH
F32, BF16 = jnp.float32, jnp.bfloat16
STEPS = (0, 1, -1, 2, -2, 3, -3, 4, -4, 5, -5, 6, -6, 7, -7, 8)
ROWS, COLUMNS = 256, 512
ORDER = (
    (0, 0), (0, 1), (1, 0), (1, 1), (0, 2), (1, 2), (2, 0), (2, 1), (2, 2),
    (3, 0), (3, 1), (3, 2), (3, 3), (0, 3), (1, 3), (2, 3),
)
QUERY_CODE = sum((3 - q) * 4**turn for turn, (q, _) in enumerate(ORDER))
KEY_CODE = sum((3 - k) * 4**turn for turn, (_, k) in enumerate(ORDER))
EARLY, LATE = (1, 2, 3, 4, 5), (9, 10, 11, 12, 13, 14, 15)
VMEM = pl.BlockSpec(memory_space=pltpu.VMEM)


def kernel(
    q_any, g_any, o_any, k_any, v_any, lse_ref, keep_ref, back_k, back_q,
    q_ref, g_ref, o_ref, k_ref, v_ref,
    keep, extra, qg, kv, qs, ks, qa, ga, qt, gt, ka, va, acc_q, acc_k, acc_v,
    part_k, got_k, part_q, got_q, pack_k, pack_q,
    load_sem, local_sem, in_send, in_recv, ring_send, ring_recv,
    sum_send, sum_recv, sumq_send, sumq_recv, out_send, out_recv,
):
    row, col = lax.axis_index("row"), lax.axis_index("col")
    high = lax.rem(col, 2)
    head = high * 8 + row
    x, y = lax.rem(lax.div(col, 2), RING), lax.div(col, 2 * RING)

    def head_device(step):
        other = lax.rem(head + step + HEADS, HEADS)
        return other, (lax.rem(other, 8), col - high + lax.div(other, 8))

    def side_device(which, step):
        if which == 0:
            return (row, col + 2 * (lax.rem(x + step + RING, RING) - x))
        return (row, col + 2 * RING * (lax.rem(y + step + RING, RING) - y))

    def remote(source, target, send, recv, device):
        return pltpu.make_async_remote_copy(
            src_ref=source, dst_ref=target, send_sem=send, recv_sem=recv,
            device_id=device, device_id_type=MESH,
        )

    def arrive(which, step):
        other, device = head_device(STEPS[step])
        source, target = ((qg, qs), (kv, ks))[which]
        return remote(
            source.at[other], target.at[0, step],
            in_send.at[which, step], in_recv.at[which, step], device,
        )

    def arrive_own(which):
        source, target = ((qg, qs), (kv, ks))[which]
        return pltpu.make_async_copy(source.at[head], target.at[0, 0], local_sem.at[which])

    def ring(which, group, kind):
        ref = (qs, ks)[which]
        source, target, first, count, step = (
            (0, 1, 0, 4, 1), (0, 2, 0, 4, -1), (1, 3, 0, 2, 1), (2, 3, 2, 2, -1),
        )[kind]
        part = pl.ds(4 * group + first, count)
        return remote(
            ref.at[source, part], ref.at[target, part],
            ring_send.at[which, group, kind], ring_recv.at[which, group, kind],
            side_device(which, step),
        )

    back_steps = (-1, 1, 2)

    def sum_keys(quarter, slot):
        return remote(
            part_k.at[quarter, slot], got_k.at[quarter, slot],
            sum_send.at[quarter, slot], sum_recv.at[quarter, slot],
            side_device(1, back_steps[slot]),
        )

    def sum_queries(quarter, slot):
        return remote(
            part_q.at[quarter, slot], got_q.at[quarter, slot],
            sumq_send.at[quarter, slot], sumq_recv.at[quarter, slot],
            side_device(0, back_steps[slot]),
        )

    def leave(which, step):
        source, target = ((pack_q, back_q), (pack_k, back_k))[which]
        if step == 0:
            return pltpu.make_async_copy(source.at[0], target.at[head], local_sem.at[2 + which])
        _, device = head_device(-STEPS[step])
        return remote(
            source.at[step], target.at[head],
            out_send.at[which, step], out_recv.at[which, step], device,
        )

    barrier = pltpu.get_barrier_semaphore()
    partners = [head_device(step)[1] for step in range(1, HEADS)]
    partners += [side_device(which, step) for which in (0, 1) for step in back_steps]
    for device in partners:
        pl.semaphore_signal(barrier, inc=1, device_id=device, device_id_type=MESH)

    loads = [
        pltpu.make_async_copy(source, target, load_sem.at[number])
        for number, (source, target) in enumerate(
            ((k_any, k_ref), (v_any, v_ref), (q_any, q_ref), (g_any, g_ref), (o_any, o_ref))
        )
    ]
    for load in loads:
        load.start()

    def flip(top, bottom):
        return jnp.concatenate([top, bottom], axis=0).astype(F32).T

    loads[0].wait()
    loads[1].wait()
    keep[...] = jnp.ones_like(keep)
    keep[0:1, :TOK] = keep_ref[...].astype(F32)
    kv[...] = (flip(k_ref[...], v_ref[...]) * keep[0:1, :]).astype(BF16).reshape(HEADS, DIM, PAIR)

    for load in loads[2:]:
        load.wait()
    qg_flat = flip(q_ref[...], g_ref[...])
    o_flat = flip(o_ref[...], o_ref[...])
    delta = jnp.sum((qg_flat * o_flat).reshape(HEADS, DIM, PAIR), axis=1)
    extra[...] = jnp.zeros_like(extra)
    extra[:, :TOK] = lse_ref[...] * (1.0 / SCALING)
    low = lax.broadcasted_iota(jnp.int32, (1, PAIR), 1) < TOK
    whole = jnp.where(low, extra[...], delta)
    first = whole.astype(BF16).astype(F32)
    second = (whole - first).astype(BF16).astype(F32)
    third = whole - first - second
    line = lax.broadcasted_iota(jnp.int32, (QROWS - DIM, PAIR), 0)
    qg[:, :DIM, :] = qg_flat.astype(BF16).reshape(HEADS, DIM, PAIR)
    for number in range(HEADS):
        rows = jnp.where(line == 0, first[number : number + 1], 0.0)
        rows = jnp.where(line == 1, second[number : number + 1], rows)
        rows = jnp.where(line == 2, third[number : number + 1], rows)
        qg[number, DIM:, :] = rows.astype(BF16)
    pl.semaphore_wait(barrier, len(partners))
    for which in (0, 1):
        arrive_own(which).start()
    for group in range(4):
        for which in (0, 1):
            for step in range(max(1, 4 * group), 4 * group + 4):
                arrive(which, step).start()

    def swap(value):
        return pltpu.roll(value, TOK, 1)

    def mix(one, two):
        return jnp.where(low, one, swap(two)), jnp.where(low, swap(one), two)

    minus = jnp.where(line < 3, -1.0, 0.0)
    fill = jnp.zeros((PAIR - QROWS, PAIR), F32)

    def lay_queries(quarter, slot):
        for pair in range(2):
            here = pl.ds(slot * QUARTER + pair * PAIR, PAIR)
            at = 4 * quarter + 2 * pair
            q, g = mix(qs[slot, at].astype(F32), qs[slot, at + 1].astype(F32))
            qt[quarter, :, here] = q[:DIM].astype(BF16)
            gt[quarter, :, here] = g[:DIM].astype(BF16)
            qa[quarter, here, :] = jnp.concatenate([q, fill], axis=0).T.astype(BF16)
            ga[quarter, here, :] = jnp.concatenate([g, fill], axis=0).T.astype(BF16)

    def lay_keys(quarter, slot):
        for pair in range(2):
            here = pl.ds(slot * QUARTER + pair * PAIR, PAIR)
            at = 4 * quarter + 2 * pair
            k, v = mix(ks[slot, at].astype(F32), ks[slot, at + 1].astype(F32))
            ka[quarter, :, here] = jnp.concatenate([k, minus, fill], axis=0).astype(BF16)
            va[quarter, :, here] = jnp.concatenate([v, minus, fill], axis=0).astype(BF16)

    def ring_one(group):
        for which in (0, 1):
            for step in range(4 * group, 4 * group + 4):
                if step == 0:
                    arrive_own(which).wait()
                else:
                    arrive(which, step).wait_recv()
            ring(which, group, 0).start()
            ring(which, group, 1).start()

    def ring_two(group):
        for which in (0, 1):
            ring(which, group, 0).wait_recv()
            ring(which, group, 2).start()
            ring(which, group, 1).wait_recv()
            ring(which, group, 3).start()

    def ring_end(group):
        for which in (0, 1):
            ring(which, group, 2).wait_recv()
            ring(which, group, 3).wait_recv()

    def lay(group, slots):
        for slot in slots:
            lay_queries(group, slot)
            lay_keys(group, slot)

    def send_keys(quarter):
        for slot in (2, 0, 1):
            here = pl.ds((slot + 1) * QUARTER, QUARTER)
            part_k[quarter, slot, 0] = acc_k[quarter, :, here].astype(BF16)
            part_k[quarter, slot, 1] = acc_v[quarter, :, here].astype(BF16)
            sum_keys(quarter, slot).start()

    def send_queries(quarter):
        for slot in (2, 0, 1):
            here = pl.ds((slot + 1) * QUARTER, QUARTER)
            part_q[quarter, slot] = acc_q[quarter, :, here].astype(BF16)
            sum_queries(quarter, slot).start()

    def return_keys(quarter):
        for slot in range(3):
            sum_keys(quarter, slot).wait_recv()
        for pair in range(2):
            here = pl.ds(pair * PAIR, PAIR)
            k, v = acc_k[quarter, :, here], acc_v[quarter, :, here]
            for slot in range(3):
                k = k + got_k[quarter, slot, 0, :, here].astype(F32)
                v = v + got_k[quarter, slot, 1, :, here].astype(F32)
            one, two = mix(k * SCALING, v)
            at = 4 * quarter + 2 * pair
            pack_k[at] = one.astype(BF16)
            pack_k[at + 1] = two.astype(BF16)
        for step in range(4 * quarter, 4 * quarter + 4):
            leave(1, step).start()

    def return_queries(quarter):
        for slot in range(3):
            sum_queries(quarter, slot).wait_recv()
        for pair in range(2):
            here = pl.ds(pair * PAIR, PAIR)
            q = acc_q[quarter, :, here]
            for slot in range(3):
                q = q + got_q[quarter, slot, :, here].astype(F32)
            q = q * SCALING
            rest = jnp.concatenate([q[TOP:], jnp.zeros((TOP - REST, PAIR), F32)], axis=0)
            one, two = mix(q[:TOP], rest)
            at = 4 * quarter + 2 * pair
            pack_q[at] = one.astype(BF16)
            pack_q[at + 1] = two.astype(BF16)
        for step in range(4 * quarter, 4 * quarter + 4):
            leave(0, step).start()

    for ref in (acc_q, acc_k, acc_v):
        ref[...] = jnp.zeros_like(ref)
    ring_one(0)
    lay(0, (0,))
    ring_two(0)
    ring_one(1)
    lay(0, (1, 2))
    ring_end(0)
    lay(0, (3,))
    ring_two(1)

    def before(turn):
        if turn == 1:
            ring_one(2)
            ring_end(1)
            lay(1, range(4))
        if turn == 2:
            ring_two(2)
        if turn == 3:
            ring_one(3)
        if turn == 4:
            ring_end(2)
            lay(2, range(4))
        if turn == 5:
            ring_two(3)
        if turn == 9:
            ring_end(3)
            lay(3, range(4))
        if turn == 10:
            send_keys(0)
        if turn == 11:
            send_keys(1)
        if turn == 12:
            send_keys(2)
            return_keys(0)
        if turn == 13:
            send_queries(3)
        if turn == 14:
            send_queries(0)
            return_keys(1)
        if turn == 15:
            send_queries(1)
            return_queries(3)

    def score(chunk):
        query, key, rows, columns = chunk
        scores = jnp.dot(qa[query, rows, :], ka[key, :, columns], preferred_element_type=F32)
        grad_probs = jnp.dot(ga[query, rows, :], va[key, :, columns], preferred_element_type=F32)
        return scores, grad_probs

    def weigh(scores, grad_probs):
        probs = jnp.exp2(scores * (SCALING * LOG2E))
        return probs.astype(BF16), (probs * grad_probs).astype(BF16)

    def gather(chunk, probs, grad_scores):
        query, key, rows, columns = chunk
        acc_v[key, :, columns] += jnp.dot(gt[query, :, rows], probs, preferred_element_type=F32)
        acc_k[key, :, columns] += jnp.dot(qt[query, :, rows], grad_scores, preferred_element_type=F32)
        acc_q[query, :, rows] += lax.dot_general(
            ka[key, :DIM, columns], grad_scores, (((1,), (1,)), ((), ())), preferred_element_type=F32
        )

    def tile(turn, codes):
        code_q, code_k = codes
        query, key = 3 - lax.rem(code_q, 4), 3 - lax.rem(code_k, 4)

        @pl.when(turn < 6)
        def _():
            for at in EARLY:
                pl.when(turn == at)(lambda at=at: before(at))

        @pl.when(turn > 8)
        def _():
            for at in LATE:
                pl.when(turn == at)(lambda at=at: before(at))

        chunks = [
            (query, key, pl.ds(at, ROWS), pl.ds(to, COLUMNS))
            for at in range(0, GROUP, ROWS)
            for to in range(0, GROUP, COLUMNS)
        ]
        ready, waiting = score(chunks[0]), None
        for number, chunk in enumerate(chunks):
            coming = score(chunks[number + 1]) if number + 1 < len(chunks) else None
            weighed = weigh(*ready)
            if waiting is not None:
                gather(chunks[number - 1], *waiting)
            waiting, ready = weighed, coming
        gather(chunks[-1], *waiting)
        return lax.div(code_q, 4), lax.div(code_k, 4)

    lax.fori_loop(0, 16, tile, (jnp.int32(QUERY_CODE), jnp.int32(KEY_CODE)))
    def settle(which, group, sent):
        for step in range(4 * group, 4 * group + 4):
            if not sent:
                leave(which, step).wait() if step == 0 else leave(which, step).wait_recv()
            elif step > 0:
                leave(which, step).wait_send()

    send_keys(3)
    send_queries(2)
    return_keys(2)
    return_queries(0)
    return_queries(1)
    for which in (0, 1):
        for step in range(1, HEADS):
            arrive(which, step).wait_send()
        for group in range(4):
            for kind in range(4):
                ring(which, group, kind).wait_send()
    for slot in range(3):
        for quarter in (0, 1, 2):
            sum_keys(quarter, slot).wait_send()
        for quarter in (0, 1, 3):
            sum_queries(quarter, slot).wait_send()
    early = ((1, 0), (1, 1), (0, 3))
    for which, group in early:
        settle(which, group, False)
        settle(which, group, True)
    return_queries(2)
    return_keys(3)

    late = ((0, 0), (0, 1), (1, 2), (0, 2), (1, 3))
    for slot in range(3):
        sum_queries(2, slot).wait_send()
        sum_keys(3, slot).wait_send()
    for sent in (True, False):
        for which, group in late:
            settle(which, group, sent)


def finish(back_k, back_q, keep_ref, dq_ref, dk_ref, dv_ref, keep):
    keep[:, :TOK] = jnp.broadcast_to(keep_ref[...].astype(F32), (8, TOK))
    keep[:, TOK:] = jnp.broadcast_to(keep_ref[...].astype(F32), (8, TOK))
    flat = (back_k[...].astype(F32).reshape(WIDTH, PAIR) * keep[0:1, :]).T
    dk_ref[...] = flat[:TOK].astype(BF16)
    dv_ref[...] = flat[TOK:].astype(BF16)
    pieces = []
    for number in range(HEADS):
        block = back_q[number].astype(F32)
        pieces += [block, pltpu.roll(block, TOK, 1)[:REST]]
    dq_ref[...] = jnp.concatenate(pieces, axis=0).T[:TOK].astype(BF16)


def on_device(query_vecs, key_vecs, value_vecs, attn_out, out_grad, saved_lse, kept_mask):
    shape = jax.ShapeDtypeStruct
    keep = kept_mask.reshape(1, TOK)
    dma = pltpu.SemaphoreType.DMA

    def low_bits(*dims):
        return pltpu.VMEM(dims, BF16)

    def full(*dims):
        return pltpu.VMEM(dims, F32)

    back = pl.pallas_call(
        kernel,
        out_shape=[shape((HEADS, DIM, PAIR), BF16), shape((HEADS, TOP, PAIR), BF16)],
        in_specs=[pl.BlockSpec(memory_space=pl.ANY)] * 5 + [VMEM] * 2,
        out_specs=[VMEM] * 2,
        scratch_shapes=[
            *[low_bits(TOK, WIDTH)] * 5,
            full(8, PAIR),
            full(HEADS, PAIR),
            low_bits(HEADS, QROWS, PAIR),
            low_bits(HEADS, DIM, PAIR),
            low_bits(RING, HEADS, QROWS, PAIR),
            low_bits(RING, HEADS, DIM, PAIR),
            low_bits(RING, GROUP, PAIR),
            low_bits(RING, GROUP, PAIR),
            low_bits(RING, DIM, GROUP),
            low_bits(RING, DIM, GROUP),
            low_bits(RING, PAIR, GROUP),
            low_bits(RING, PAIR, GROUP),
            full(RING, DIM, GROUP),
            full(RING, DIM, GROUP),
            full(RING, DIM, GROUP),
            low_bits(RING, 3, 2, DIM, QUARTER),
            low_bits(RING, 3, 2, DIM, QUARTER),
            low_bits(RING, 3, DIM, QUARTER),
            low_bits(RING, 3, DIM, QUARTER),
            low_bits(HEADS, DIM, PAIR),
            low_bits(HEADS, TOP, PAIR),
            dma((5,)),
            dma((4,)),
            dma((2, HEADS)),
            dma((2, HEADS)),
            dma((2, 4, 4)),
            dma((2, 4, 4)),
            dma((4, 3)),
            dma((4, 3)),
            dma((4, 3)),
            dma((4, 3)),
            dma((2, HEADS)),
            dma((2, HEADS)),
        ],
        compiler_params=pltpu.CompilerParams(
            vmem_limit_bytes=56 * 2**20, collective_id=0, has_side_effects=True
        ),
    )(
        query_vecs, out_grad, attn_out, key_vecs, value_vecs, saved_lse.T, keep,
    )
    return pl.pallas_call(
        finish,
        out_shape=[shape((TOK, WIDTH), BF16)] * 3,
        in_specs=[VMEM] * 3,
        out_specs=[VMEM] * 3,
        scratch_shapes=[full(8, PAIR)],
    )(*back, keep)


def solution(mesh):
    queries, keys = P(("row", "col"), None), P(("col", "row"), None)
    return jax.shard_map(
        on_device,
        mesh=mesh,
        in_specs=(queries, keys, keys, queries, queries, queries, P(("col", "row"))),
        out_specs=(queries, keys, keys),
        check_vma=False,
    )
```
